128 devices in a mesh: section: 8 (over x, y_lo), expert: 16 (over y_hi, z, core).
Axes of the slice: x: 4, y: 4 (y_hi: 2, y_lo: 2; y = y_hi * 2 + y_lo), z: 4, core: 2. Of those that a mesh axis runs over, the one named last changes fastest.
Arguments:
- x_fwd: bfloat16 [8, 1024, 7168], P('section', 'expert'), may hold values from -6 to 6
- routes_fwd: int32 [8, 1024, 2], P('section', 'expert'), may hold values from 0 to 3, as said below
- slots_fwd: int32 [8, 1024, 2], P('section', 'expert'), may hold values from 0 to 35, as said below
- logits_fwd: float32 [8, 1024, 2], P('section', 'expert'), may hold values from -6 to 6
- x_bwd: bfloat16 [8, 1024, 7168], P('section', 'expert'), may hold values from -6 to 6
- cot_bwd: bfloat16 [8, 1024, 7168], P('section', 'expert'), may hold values from -6 to 6
- routes_bwd: int32 [8, 1024, 2], P('section', 'expert'), may hold values from 0 to 3, as said below
- slots_bwd: int32 [8, 1024, 2], P('section', 'expert'), may hold values from 0 to 35, as said below
- logits_bwd: float32 [8, 1024, 2], P('section', 'expert'), may hold values from -6 to 6
- gain: float32 [8, 7168], P('section'), may hold values from 0.5 to 1.5
- w_gate: bfloat16 [8, 7168, 8192], P('section', None, 'expert'), may hold values from -0.0625 to 0.0625
- w_up: bfloat16 [8, 7168, 8192], P('section', None, 'expert'), may hold values from -0.0625 to 0.0625
- w_down: bfloat16 [8, 8192, 7168], P('section', 'expert'), may hold values from -0.125 to 0.125
Outputs:
- fwd_arrived: bfloat16 [8, 1024, 7168], P('section', 'expert')
- grad_arrived: bfloat16 [8, 1024, 7168], P('section', 'expert')
The draws below stay inside these ranges and needn't reach their ends.
Inputs may be any that keep to these rules, and one draw needn't show every extreme that they name: `routes_fwd`: in each aligned block of 64 rows (the tokens of one index of expert in one layer) a token names 2 different experts, no expert is named by more than 36 tokens, and one expert by exactly 36. `slots_fwd`: an assignment's slot is the number of earlier tokens of its aligned block of 64 rows that name the same expert. `routes_bwd`: as for routes_fwd. `slots_bwd`: as for slots_fwd.
All inputs are finite; a program needn't handle non-finite values.
Results may differ from the reference program's by a relative error of at most 0.0069.
Values may be sent and summed in bfloat16 or wider, within the bound.
A program may use at most 192 MiB of HBM per device.

```python
import jax
import jax.numpy as jnp
from jax import lax

D = 7168
FF = 2048
EXP_WIN = 4
TOPK = 2
TOK = 64
CAP = 36
TOKENS = 1024
GROUP = 4
HID = 512
N_SECTION = 8
N_EXPERT = 16


def route_table(key):
    blocks_count = N_SECTION * (TOKENS // TOK)
    block_keys = jax.random.split(key, blocks_count)
    others_count = EXP_WIN - 1

    def one_block(block_key):
        key_order, key_hot, key_rest = jax.random.split(block_key, 3)
        position = jnp.argsort(jax.random.permutation(key_order, TOK)).astype(jnp.int32)
        hot_expert = jax.random.randint(key_hot, (), 0, EXP_WIN).astype(jnp.int32)
        rest_order = jax.random.permutation(key_rest, others_count).astype(jnp.int32)
        others = (hot_expert + 1 + rest_order) % EXP_WIN
        later = position - CAP
        first_pick = jnp.where(position < CAP, hot_expert, others[later % others_count])
        second_pick = jnp.where(position < CAP, others[position % others_count], others[(later + 1) % others_count])
        picks = jnp.stack([first_pick, second_pick], axis=-1).astype(jnp.int32)
        onehot = jnp.sum((picks[:, :, None] == jnp.arange(EXP_WIN, dtype=jnp.int32)[None, None, :]).astype(jnp.int32), axis=1)
        earlier = jnp.cumsum(onehot, axis=0) - onehot
        slot_ids = jnp.take_along_axis(earlier, picks, axis=1).astype(jnp.int32)
        return (picks, slot_ids)
    picks_all, slots_all = jax.vmap(one_block)(block_keys)
    return (picks_all.reshape(N_SECTION, TOKENS, TOPK), slots_all.reshape(N_SECTION, TOKENS, TOPK))


def draw_routes_fwd(key, part):
    return route_table(jax.random.fold_in(key, 11))[0]


def draw_slots_fwd(key, part):
    return route_table(jax.random.fold_in(key, 11))[1]


def draw_routes_bwd(key, part):
    return route_table(jax.random.fold_in(key, 12))[0]


def draw_slots_bwd(key, part):
    return route_table(jax.random.fold_in(key, 12))[1]


def levels(stream_key, shape, pieces, low, high):
    def one(dim, parts):
        steps = jax.random.uniform(jax.random.fold_in(jax.random.fold_in(stream_key, 6), dim), (parts,), jnp.float32, low / len(pieces), high / len(pieces))
        return jnp.repeat(jnp.exp(steps), shape[dim] // parts).reshape((-1,) + (1,) * (len(shape) - dim - 1))

    factor_of = one(*pieces[0])
    for cut in pieces[1:]:
        factor_of = factor_of * one(*cut)
    return factor_of


def centred(rng, shape, spread, reach, shards=(), kind=jnp.bfloat16):
    values = spread * jax.random.normal(rng, shape, jnp.float32)
    if shards:
        values = values * levels(rng, shape, shards, -0.22, 0.18)
    return jnp.clip(values, -reach, reach).astype(kind)


def setup_inputs(seed: int = 0) -> dict:
    keys = jax.random.split(jax.random.key(seed), 14)
    x_fwd = centred(keys[0], (N_SECTION, TOKENS, D), 1.0, 6.0, ((0, 8), (1, 16)))
    routes_fwd = draw_routes_fwd(jax.random.fold_in(keys[13], 71), 0)
    slots_fwd = draw_slots_fwd(jax.random.fold_in(keys[13], 71), 0)
    logits_fwd = centred(keys[3], (N_SECTION, TOKENS, TOPK), 1.5, 6.0, ((0, 8), (1, 16)), jnp.float32)
    x_bwd = centred(keys[4], (N_SECTION, TOKENS, D), 1.0, 6.0, ((0, 8), (1, 16)))
    cot_bwd = centred(keys[5], (N_SECTION, TOKENS, D), 1.0, 6.0, ((0, 8), (1, 16)))
    routes_bwd = draw_routes_bwd(jax.random.fold_in(keys[13], 71), 0)
    slots_bwd = draw_slots_bwd(jax.random.fold_in(keys[13], 71), 0)
    logits_bwd = centred(keys[8], (N_SECTION, TOKENS, TOPK), 1.5, 6.0, ((0, 8), (1, 16)), jnp.float32)
    gain = jnp.clip(1.0 + 0.1 * jax.random.normal(keys[9], (N_SECTION, D), jnp.float32), 0.5, 1.5)
    w_gate = centred(keys[10], (N_SECTION, D, EXP_WIN * FF), D ** -0.5, 0.0625, ((0, 8), (2, 16)))
    w_up = centred(keys[11], (N_SECTION, D, EXP_WIN * FF), D ** -0.5, 0.0625, ((0, 8), (2, 16)))
    w_down = centred(keys[12], (N_SECTION, EXP_WIN * FF, D), FF ** -0.5, 0.125, ((0, 8), (1, 16)))
    return dict(x_fwd=x_fwd, routes_fwd=routes_fwd, slots_fwd=slots_fwd, logits_fwd=logits_fwd, x_bwd=x_bwd, cot_bwd=cot_bwd, routes_bwd=routes_bwd, slots_bwd=slots_bwd, logits_bwd=logits_bwd, gain=gain, w_gate=w_gate, w_up=w_up, w_down=w_down)


epsilon = 1e-06
route_scale = 2.5

def normalize(inputs, gain_row):
    widened = inputs.astype(jnp.float32)
    inverse = lax.rsqrt(lax.optimization_barrier(jnp.mean(widened * widened, axis=-1, keepdims=True)) + epsilon)
    normed = (widened * inverse * gain_row[None, :]).astype(jnp.bfloat16)
    return (widened, inverse, normed)

def mixing(logits):
    affinity = jax.nn.sigmoid(logits)
    return route_scale * affinity / lax.optimization_barrier(jnp.sum(affinity, axis=-1, keepdims=True))

def layout(routes, slots):
    source = jnp.arange(TOKENS, dtype=jnp.int32) // TOK
    flat_index = (routes * N_EXPERT + source[:, None]) * CAP + slots
    columns = flat_index.reshape(-1)
    matches = columns[None, :] == jnp.arange(EXP_WIN * N_EXPERT * CAP, dtype=jnp.int32)[:, None]
    token_ids = jnp.arange(columns.shape[0], dtype=jnp.int32) // TOPK
    owner = lax.optimization_barrier(jnp.sum(jnp.where(matches, token_ids[None, :], 0), axis=1)).astype(jnp.int32)
    filled = jnp.any(matches, axis=1)
    return (flat_index, matches, owner, filled)

def rounded(values):
    return lax.optimization_barrier(values.astype(jnp.bfloat16)).astype(jnp.float32)

def forward_section(inputs, routes, slots, logits, gain_row, gate_w, up_w, down_w):
    widened, inverse, normed = normalize(inputs, gain_row)
    shares = mixing(logits)
    flat_index, matches, owner, filled = layout(routes, slots)
    blocks = jnp.where(filled[:, None], normed[owner], jnp.zeros((), jnp.bfloat16))
    blocks = blocks.reshape(EXP_WIN, N_EXPERT * CAP, D)
    outputs = []
    for expert in range(EXP_WIN):
        first = expert * FF
        gate_pre = jnp.dot(blocks[expert], gate_w[:, first:first + FF], preferred_element_type=jnp.float32)
        up_pre = jnp.dot(blocks[expert], up_w[:, first:first + FF], preferred_element_type=jnp.float32)
        hidden = (jax.nn.silu(gate_pre) * up_pre).astype(jnp.bfloat16)
        total = jnp.zeros((N_EXPERT * CAP, D), jnp.float32)
        for quarter in range(GROUP):
            offset = quarter * HID
            piece = jnp.dot(hidden[:, offset:offset + HID], down_w[first + offset:first + offset + HID], preferred_element_type=jnp.float32)
            total = total + rounded(piece)
        outputs.append(total)
    mixed = jnp.concatenate(outputs, axis=0)
    picked = mixed[flat_index]
    return (widened + lax.optimization_barrier(jnp.sum(shares[:, :, None] * picked, axis=1))).astype(jnp.bfloat16)

def backward_section(inputs, cotangent, routes, slots, logits, gain_row, gate_w, up_w, down_w):
    widened, inverse, normed = normalize(inputs, gain_row)
    shares = mixing(logits)
    flat_index, matches, owner, filled = layout(routes, slots)
    blocks = jnp.where(filled[:, None], normed[owner], jnp.zeros((), jnp.bfloat16))
    blocks = blocks.reshape(EXP_WIN, N_EXPERT * CAP, D)
    weight_row = lax.optimization_barrier(jnp.sum(jnp.where(matches, shares.reshape(-1)[None, :], jnp.zeros((), jnp.float32)), axis=1))
    cot_rows = (cotangent[owner].astype(jnp.float32) * weight_row[:, None]).astype(jnp.bfloat16)
    cot_rows = cot_rows.reshape(EXP_WIN, N_EXPERT * CAP, D)
    outputs = []
    for expert in range(EXP_WIN):
        first = expert * FF
        gate_block = gate_w[:, first:first + FF]
        up_block = up_w[:, first:first + FF]
        gate_pre = jnp.dot(blocks[expert], gate_block, preferred_element_type=jnp.float32)
        up_pre = jnp.dot(blocks[expert], up_block, preferred_element_type=jnp.float32)
        sigma = jax.nn.sigmoid(gate_pre)
        d_hidden = jnp.dot(cot_rows[expert], down_w[first:first + FF].T, preferred_element_type=jnp.float32)
        d_gate = (d_hidden * up_pre * sigma * (1.0 + gate_pre * (1.0 - sigma))).astype(jnp.bfloat16)
        d_up = (d_hidden * gate_pre * sigma).astype(jnp.bfloat16)
        total = jnp.zeros((N_EXPERT * CAP, D), jnp.float32)
        for quarter in range(GROUP):
            offset = quarter * HID
            piece = jnp.dot(d_gate[:, offset:offset + HID], gate_block[:, offset:offset + HID].T, preferred_element_type=jnp.float32)
            piece = piece + jnp.dot(d_up[:, offset:offset + HID], up_block[:, offset:offset + HID].T, preferred_element_type=jnp.float32)
            total = total + rounded(piece)
        outputs.append(total)
    d_mixed = jnp.concatenate(outputs, axis=0)
    d_normed = lax.optimization_barrier(jnp.sum(d_mixed[flat_index], axis=1))
    scaled = gain_row[None, :] * d_normed
    along = lax.optimization_barrier(jnp.sum(widened * scaled, axis=-1, keepdims=True)) / D
    d_inputs = cotangent.astype(jnp.float32) + inverse * scaled - widened * inverse * inverse * inverse * along
    return d_inputs.astype(jnp.bfloat16)

def reference(x_fwd, routes_fwd, slots_fwd, logits_fwd, x_bwd, cot_bwd, routes_bwd, slots_bwd, logits_bwd, gain, w_gate, w_up, w_down):
    forward_out = []
    backward_out = []
    for section in range(N_SECTION):
        forward_out.append(forward_section(x_fwd[section], routes_fwd[section], slots_fwd[section], logits_fwd[section], gain[section], w_gate[section], w_up[section], w_down[section]))
        backward_out.append(backward_section(x_bwd[section], cot_bwd[section], routes_bwd[section], slots_bwd[section], logits_bwd[section], gain[section], w_gate[section], w_up[section], w_down[section]))
    forward_all = jnp.stack(forward_out, axis=0)
    backward_all = jnp.stack(backward_out, axis=0)
    return (jnp.roll(forward_all, 1, axis=0), jnp.roll(backward_all, -1, axis=0))
```

```python
import jax
import jax.numpy as jnp
from jax import lax
from jax.experimental import pallas as pl
from jax.experimental.pallas import tpu as pltpu
from jax.sharding import PartitionSpec as P

D = 7168
EXP_WIN = 4
TOPK = 2
CAP = 36
TOK = 64
HID = 512
PAIR = 4 * CAP
SLOTS = EXP_WIN * PAIR
CH = 896
NK = 4
NKK = 2 * NK

epsilon = 1e-06
route_scale = 2.5
MESH = pl.DeviceIdType.MESH
BF = jnp.bfloat16
F32 = jnp.float32


class Place:
    def __init__(self):
        me = lax.axis_index("expert")
        self.core = lax.rem(me, 2)
        z = lax.rem(me // 2, 4)
        a = me // 8
        b = z // 2
        zl = lax.rem(z, 2)
        self.h = b + zl - 2 * b * zl
        zg = z + 1 - 2 * zl

        def at(a_, z_, c_):
            return a_ * 8 + z_ * 2 + c_

        self.mate = at(a, z, 1 - self.core)
        self.g = at(a, zg, self.core)
        self.gmate = at(a, zg, 1 - self.core)
        self.c = at(a, 3 - z, self.core)
        self.y = at(1 - a, z, self.core)
        self.pairs = (a * 2 + b, a * 2 + 1 - b, (1 - a) * 2 + b, (1 - a) * 2 + 1 - b)
        self.index = self.h * 2 + self.core


class Copies:
    def __init__(self, sems):
        self.sems = sems
        self.used = 0

    def sem(self):
        self.used += 1
        return self.sems.at[self.used - 1]

    def remote(self, src, dst, device, axis="expert"):
        copy = pltpu.make_async_remote_copy(
            src_ref=src,
            dst_ref=dst,
            send_sem=self.sem(),
            recv_sem=self.sem(),
            device_id={axis: device},
            device_id_type=MESH,
        )
        copy.start()
        return copy

    def local(self, src, dst):
        copy = pltpu.make_async_copy(src, dst, self.sem())
        copy.start()
        return copy


def greet(places, others=()):
    barrier = pltpu.get_barrier_semaphore()
    for place in places:
        pl.semaphore_signal(barrier, inc=1, device_id={"expert": place}, device_id_type=MESH)
    for place in others:
        pl.semaphore_signal(barrier, inc=1, device_id={"section": place}, device_id_type=MESH)
    pl.semaphore_wait(barrier, len(places) + len(others))


def rows64(first):
    return pl.ds(pl.multiple_of(first, 64), 64)


def rows128(first):
    return pl.ds(pl.multiple_of(first, 128), 128)


def rows144(pair):
    return pl.ds(pl.multiple_of(pair * PAIR, PAIR), PAIR)


def dispatch_kernel(
    xf, xb, cot, gain, meta, rows, metas_out,
    hbuf, tok, stage, relay, metas, place_m, sems,
):
    at = Place()
    cp = Copies(sems)
    greet((at.mate, at.g, at.gmate, at.c, at.y))
    h, core = at.h, at.core
    half = core * NK
    other = (1 - core) * NK
    mine = metas.at[at.index]
    meta_sends = [cp.remote(meta, mine, d) for d in (at.mate, at.g, at.gmate)]
    metas[at.index] = meta[...]

    my_rows = h * 128 + core * 64
    tok_in = []
    for t, src in enumerate((xf, xb, cot)):
        if t < 2:
            total = jnp.zeros((TOK, 1), F32)
            for kk in range(NKK):
                v = src[:, kk * CH:(kk + 1) * CH].astype(F32)
                total = total + jnp.sum(v * v, axis=-1, keepdims=True)
            inverse = lax.rsqrt(total / D + epsilon)
        for kk in range(NKK):
            v = src[:, kk * CH:(kk + 1) * CH]
            if t < 2:
                v = (v.astype(F32) * inverse * gain[:, kk * CH:(kk + 1) * CH]).astype(BF)
            hbuf[t, kk] = v
        tok_in.append(cp.remote(
            hbuf.at[t, pl.ds(other, NK)], tok.at[t, :, rows64(my_rows), :], at.mate))
        for k in range(NK):
            tok[t, k, rows64(my_rows), :] = hbuf[t, half + k]

    steps = [(t, i) for t in range(3) for i in range(NK)]
    n = len(steps)
    tok_g = {}

    def send_tokens(s):
        if s >= n:
            return
        t, i = steps[s]
        if i == 0:
            tok_in[t].wait_recv()
        q = lax.rem(2 * (1 - h) + i, NK)
        piece = tok.at[t, q, rows128(h * 128), :]
        tok_g[s] = cp.remote(piece, piece, at.g)

    for s in range(3):
        send_tokens(s)

    for m in meta_sends:
        m.wait_recv()
    for fb in range(2):
        for rel in range(4):
            first = at.pairs[rel] * PAIR
            ids = (lax.broadcasted_iota(jnp.int32, (PAIR, 128), 0) + first).astype(F32)
            for hh in range(2):
                m = metas[2 * hh] + metas[2 * hh + 1]
                k0 = m[fb * 8:fb * 8 + 1, :]
                k1 = m[fb * 8 + 1:fb * 8 + 2, :]
                hit = jnp.where(ids == k0, 1.0, 0.0) + jnp.where(ids == k1, 1.0, 0.0)
                place_m[fb, rel, :, hh * 128:(hh + 1) * 128] = hit.astype(BF)
    metas_out[...] = metas[...]

    sent = {}
    moved = {}
    passed = {}
    mate_in = []

    def gather(s):
        t, i = steps[s]
        slot = s % 3
        if s >= 3:
            for key in [k for k in list(sent) if k[0] == s - 3]:
                sent[key].wait_send()
            moved[s - 3].wait()
        tok_g[s].wait_recv()
        q = lax.rem(2 * h + i, NK)
        fb = 0 if t == 0 else 1
        block = tok[t, q]
        order = (3, 2, 1, 0) if i < 2 else (2, 1, 0)
        for rel in order:
            stage[slot, rel] = jnp.dot(
                place_m[fb, rel], block, preferred_element_type=F32).astype(BF)
            src = stage.at[slot, rel]
            target = rows.at[t, half + q, rows144(at.pairs[0]), :]
            if rel == 3:
                sent[s, 3] = cp.remote(src, relay.at[t, i], at.y)
            elif rel == 2:
                sent[s, 2] = cp.remote(src, target, at.y)
            elif rel == 1:
                sent[s, 1] = cp.remote(src, target, at.c)
            else:
                moved[s] = cp.local(src, target)
                sent[s, 0] = cp.remote(src, target, at.mate)
                mate_in.append(sent[s, 0])

    def to_mate(t, chunk, pair):
        piece = rows.at[t, half + chunk, rows144(pair), :]
        copy = cp.remote(piece, piece, at.mate)
        mate_in.append(copy)
        passed[len(passed)] = copy

    def relay_first(s):
        if not 0 <= s < n or steps[s][1] >= 2:
            return
        t, i = steps[s]
        sent[s, 3].wait_recv()
        passed["c", s] = cp.remote(
            relay.at[t, i], rows.at[t, half + 2 * h + i, rows144(at.pairs[2]), :], at.c)

    def relay_second(s):
        if not 0 <= s < n or steps[s][1] >= 2:
            return
        t, i = steps[s]
        passed["c", s].wait_recv()
        piece = rows.at[t, half + 2 * h + i, rows144(at.pairs[3]), :]
        passed["g", s] = cp.remote(piece, piece, at.g)
        to_mate(t, 2 * h + i, at.pairs[3])

    def relay_last(s):
        if not 0 <= s < n or steps[s][1] >= 2:
            return
        t, i = steps[s]
        passed["g", s].wait_recv()
        to_mate(t, 2 * (1 - h) + i, at.pairs[3])

    def pass_on(s):
        if not 0 <= s < n:
            return
        t, i = steps[s]
        q = lax.rem(2 * h + i, NK)
        sent[s, 2].wait_recv()
        to_mate(t, q, at.pairs[2])
        sent[s, 1].wait_recv()
        to_mate(t, q, at.pairs[1])

    for s in range(n + 3):
        send_tokens(s + 3)
        if s < n:
            gather(s)
        relay_first(s - 1)
        relay_second(s - 2)
        pass_on(s - 1)
        relay_last(s - 3)

    for m in meta_sends + tok_in + list(tok_g.values()) + list(passed.values()):
        m.wait_send()
    for (s, rel), m in sent.items():
        if s >= n - 3:
            m.wait_send()
    for s in range(n - 3, n):
        moved[s].wait()
    for m in mate_in:
        m.wait_recv()


def dispatch(x_fwd, x_bwd, cot, gain, meta):
    vmem = pl.BlockSpec(memory_space=pltpu.VMEM)
    return pl.pallas_call(
        dispatch_kernel,
        out_shape=(
            jax.ShapeDtypeStruct((3, NKK, SLOTS, CH), BF),
            jax.ShapeDtypeStruct((4, 16, 128), F32),
        ),
        in_specs=[vmem] * 5,
        out_specs=(pl.BlockSpec(memory_space=pl.ANY), vmem),
        scratch_shapes=[
            pltpu.VMEM((3, NKK, TOK, CH), BF),
            pltpu.VMEM((3, NK, 256, CH), BF),
            pltpu.VMEM((3, 4, PAIR, CH), BF),
            pltpu.VMEM((3, 2, PAIR, CH), BF),
            pltpu.VMEM((4, 16, 128), F32),
            pltpu.VMEM((2, 4, PAIR, 256), BF),
            pltpu.SemaphoreType.DMA((260,)),
        ],
        compiler_params=pltpu.CompilerParams(
            collective_id=1, has_side_effects=True, vmem_limit_bytes=60 * 2 ** 20),
        name="dispatch",
    )(x_fwd, x_bwd, cot, gain, meta)


def forward_hidden_kernel(rows, wg, wu, act, gate, up):
    k = pl.program_id(0)

    @pl.when(k == 0)
    def _():
        gate[...] = jnp.zeros_like(gate)
        up[...] = jnp.zeros_like(up)

    r = rows[0, 0]
    gate[...] += jnp.dot(r, wg[...], preferred_element_type=F32)
    up[...] += jnp.dot(r, wu[...], preferred_element_type=F32)

    @pl.when(k == NKK - 1)
    def _():
        g = gate[...]
        act[...] = (g * jax.nn.sigmoid(g) * up[...]).astype(BF)


def forward_out_kernel(act, wd, out):
    out[0] = jnp.dot(act[...], wd[...], preferred_element_type=F32).astype(BF)


CONTRACT = (((1,), (1,)), ((), ()))


def backward_hidden_kernel(rows, cots, wg, wu, wd, dg, du, gate, up, dact):
    k = pl.program_id(0)

    @pl.when(k == 0)
    def _():
        gate[...] = jnp.zeros_like(gate)
        up[...] = jnp.zeros_like(up)
        dact[...] = jnp.zeros_like(dact)

    r = rows[0, 0]
    gate[...] += jnp.dot(r, wg[...], preferred_element_type=F32)
    up[...] += jnp.dot(r, wu[...], preferred_element_type=F32)
    dact[...] += lax.dot_general(cots[0, 0], wd[...], CONTRACT, preferred_element_type=F32)

    @pl.when(k == NKK - 1)
    def _():
        g = gate[...]
        s = jax.nn.sigmoid(g)
        d = dact[...]
        dg[...] = (d * up[...] * s * (1.0 + g * (1.0 - s))).astype(BF)
        du[...] = (d * g * s).astype(BF)


def backward_out_kernel(dg, du, wg, wu, out):
    v = lax.dot_general(dg[...], wg[...], CONTRACT, preferred_element_type=F32)
    v = v + lax.dot_general(du[...], wu[...], CONTRACT, preferred_element_type=F32)
    out[0] = v.astype(BF)


def experts(rows, wg, wu, wd):
    def rows_of(t):
        return pl.BlockSpec((1, 1, SLOTS, CH), lambda k: (t, k, 0, 0))

    tall = pl.BlockSpec((CH, HID), lambda k: (k, 0))
    wide = pl.BlockSpec((HID, CH), lambda k: (0, k))
    hidden = pl.BlockSpec((SLOTS, HID), lambda k: (0, 0))
    out = pl.BlockSpec((1, SLOTS, CH), lambda k: (k, 0, 0))
    hidden_shape = jax.ShapeDtypeStruct((SLOTS, HID), BF)
    out_shape = jax.ShapeDtypeStruct((NKK, SLOTS, CH), BF)
    acc = pltpu.VMEM((SLOTS, HID), F32)
    params = pltpu.CompilerParams(vmem_limit_bytes=60 * 2 ** 20)
    act = pl.pallas_call(
        forward_hidden_kernel, grid=(NKK,), out_shape=hidden_shape,
        in_specs=[rows_of(0), tall, tall], out_specs=hidden,
        scratch_shapes=[acc, acc], compiler_params=params, name="forward_hidden",
    )(rows, wg, wu)
    forward = pl.pallas_call(
        forward_out_kernel, grid=(NKK,), out_shape=out_shape,
        in_specs=[hidden, wide], out_specs=out, compiler_params=params, name="forward_out",
    )(act, wd)
    dg, du = pl.pallas_call(
        backward_hidden_kernel, grid=(NKK,), out_shape=(hidden_shape, hidden_shape),
        in_specs=[rows_of(1), rows_of(2), tall, tall, wide], out_specs=(hidden, hidden),
        scratch_shapes=[acc, acc, acc], compiler_params=params, name="backward_hidden",
    )(rows, rows, wg, wu, wd)
    backward = pl.pallas_call(
        backward_out_kernel, grid=(NKK,), out_shape=out_shape,
        in_specs=[hidden, hidden, tall, tall], out_specs=out, compiler_params=params,
        name="backward_out",
    )(dg, du, wg, wu)
    return forward, backward


def return_kernel(
    of, ob, xf, xb, cot, gain, metas, yf_out, dx_out,
    own, part, total, from_y, from_c, from_g, pass_y, from_yc, comb_own, comb_out, comb_in,
    spread, acc, result, meta_t, weights, sems,
):
    at = Place()
    cp = Copies(sems)
    me_s = lax.axis_index("section")
    up_s = lax.rem(me_s + 1, 8)
    down_s = lax.rem(me_s + 7, 8)
    greet((at.mate, at.g, at.c, at.y), (up_s, down_s))
    h, core = at.h, at.core
    half = core * NK
    other = (1 - core) * NK
    steps = [(t, i) for t in range(2) for i in range(NK)]
    n = len(steps)

    def chunk(i):
        return lax.rem(2 * (1 - h) + i, NK)

    outs = (of, ob)
    parts = []
    for s, (t, i) in enumerate(steps):
        q = chunk(i)
        parts.append(cp.remote(outs[t].at[other + q], part.at[t, q], at.mate))

    loads = {}

    def load(s):
        if s < n:
            t, i = steps[s]
            loads[s] = cp.local(outs[t].at[half + chunk(i)], own.at[s % 2])

    load(0)
    load(1)

    meta_t[...] = jnp.zeros_like(meta_t)
    for w in range(2):
        hh = h if w == 0 else 1 - h
        meta_t[0:16, :] = metas[2 * hh] + metas[2 * hh + 1]
        m = jnp.transpose(meta_t[...])
        for fb in range(2):
            for rel in range(4):
                first = at.pairs[rel] * PAIR
                ids = (lax.broadcasted_iota(jnp.int32, (128, PAIR), 1) + first).astype(F32)
                c = fb * 8
                v = jnp.where(ids == m[:, c:c + 1], m[:, c + 2:c + 3], 0.0)
                v = v + jnp.where(ids == m[:, c + 1:c + 2], m[:, c + 3:c + 4], 0.0)
                high = v.astype(BF)
                weights[fb, rel, 0, w * 128:(w + 1) * 128, :] = high
                weights[fb, rel, 1, w * 128:(w + 1) * 128, :] = (v - high.astype(F32)).astype(BF)

    sent = {}

    def add_up(s):
        t, i = steps[s]
        q = chunk(i)
        loads[s].wait()
        parts[s].wait_recv()
        total[t, q] = (own[s % 2].astype(F32) + part[t, q].astype(F32)).astype(BF)
        load(s + 2)

        def piece(rel):
            return total.at[t, q, rows144(at.pairs[rel]), :]

        if i < 2:
            sent["g", s] = cp.remote(piece(3), from_g.at[t, i], at.g)
        else:
            sent["g", s - 2].wait_recv()
            pass_y[t, i - 2] = (
                total[t, q, rows144(at.pairs[3]), :].astype(F32) + from_g[t, i - 2].astype(F32)
            ).astype(BF)
            sent["yg", s] = cp.remote(pass_y.at[t, i - 2], from_yc.at[t, i - 2, 0], at.c)
        sent["y", s] = cp.remote(piece(2), from_y.at[t, q], at.y)
        sent["c", s] = cp.remote(piece(1), from_c.at[t, q], at.c)

    def relay(s):
        if not 0 <= s < n or steps[s][1] < 2:
            return
        t, i = steps[s]
        sent["yg", s].wait_recv()
        sent["ygy", s] = cp.remote(from_yc.at[t, i - 2, 0], from_yc.at[t, i - 2, 1], at.y)

    def combine(s):
        if not 0 <= s < n:
            return
        t, i = steps[s]
        q = chunk(i)
        sent["y", s].wait_recv()
        sent["c", s].wait_recv()
        terms = [
            (0, total[t, q, rows144(at.pairs[0]), :]),
            (1, from_c[t, q]),
            (2, from_y[t, q]),
        ]
        if i >= 2:
            sent["ygy", s].wait_recv()
            terms.append((3, from_yc[t, i - 2, 1]))
        v = jnp.zeros((256, CH), F32)
        for rel, r in terms:
            v = v + jnp.dot(weights[t, rel, 0], r, preferred_element_type=F32)
            v = v + jnp.dot(weights[t, rel, 1], r, preferred_element_type=F32)
        comb_own[t, q] = v[0:128]
        comb_out[t, q] = v[128:256].astype(BF)
        sent["u", s] = cp.remote(comb_out.at[t, q], comb_in.at[t, q], at.g)

    def finish(s):
        t, i = steps[s]
        q = chunk(i)
        sent["u", t * NK + (i + 2) % NK].wait_recv()
        v = comb_own[t, q] + comb_in[t, q].astype(F32)
        spread[t, q, 0] = v[0:64]
        spread[t, q, 1] = v[64:128]
        sent["d", s] = cp.remote(spread.at[t, q, 1 - core], acc.at[t, half + q], at.mate)
        acc[t, half + q] = spread[t, q, core]

    def finalize(t):
        for i in range(NK):
            sent["d", t * NK + i].wait_recv()
        if t == 0:
            for kk in range(NKK):
                cols = slice(kk * CH, (kk + 1) * CH)
                result[0, :, cols] = (xf[:, cols].astype(F32) + acc[0, kk]).astype(BF)
            sent["s", 0] = cp.remote(result.at[0], yf_out, up_s, "section")
        else:
            total_sq = jnp.zeros((TOK, 1), F32)
            along = jnp.zeros((TOK, 1), F32)
            for kk in range(NKK):
                cols = slice(kk * CH, (kk + 1) * CH)
                x = xb[:, cols].astype(F32)
                total_sq = total_sq + jnp.sum(x * x, axis=-1, keepdims=True)
                along = along + jnp.sum(x * (gain[:, cols] * acc[1, kk]), axis=-1, keepdims=True)
            inverse = lax.rsqrt(total_sq / D + epsilon)
            factor = inverse * inverse * inverse * (along / D)
            for kk in range(NKK):
                cols = slice(kk * CH, (kk + 1) * CH)
                x = xb[:, cols].astype(F32)
                v = cot[:, cols].astype(F32) + inverse * (gain[:, cols] * acc[1, kk]) - x * factor
                result[1, :, cols] = v.astype(BF)
            sent["s", 1] = cp.remote(result.at[1], dx_out, down_s, "section")

    for s in range(n + 4):
        if s < n:
            add_up(s)
        relay(s - 1)
        combine(s - 2)
        if s - 2 == NK - 1:
            for i in range(NK):
                finish(i)
        if s - 3 == NK - 1:
            finalize(0)
        if s - 2 == n - 1:
            for i in range(NK):
                finish(NK + i)
    finalize(1)
    for m in parts:
        m.wait_send()
    for m in sent.values():
        m.wait_send()
    for t in range(2):
        sent["s", t].wait_recv()


def give_back(forward, backward, x_fwd, x_bwd, cot, gain, metas):
    vmem = pl.BlockSpec(memory_space=pltpu.VMEM)
    hbm = pl.BlockSpec(memory_space=pl.ANY)
    return pl.pallas_call(
        return_kernel,
        out_shape=(jax.ShapeDtypeStruct((TOK, D), BF),) * 2,
        in_specs=[hbm, hbm] + [vmem] * 5,
        out_specs=(hbm, hbm),
        scratch_shapes=[
            pltpu.VMEM((2, SLOTS, CH), BF),
            pltpu.VMEM((2, NK, SLOTS, CH), BF),
            pltpu.VMEM((2, NK, SLOTS, CH), BF),
            pltpu.VMEM((2, NK, PAIR, CH), BF),
            pltpu.VMEM((2, NK, PAIR, CH), BF),
            pltpu.VMEM((2, 2, PAIR, CH), BF),
            pltpu.VMEM((2, 2, PAIR, CH), BF),
            pltpu.VMEM((2, 2, 2, PAIR, CH), BF),
            pltpu.VMEM((2, NK, 128, CH), F32),
            pltpu.VMEM((2, NK, 128, CH), BF),
            pltpu.VMEM((2, NK, 128, CH), BF),
            pltpu.VMEM((2, NK, 2, TOK, CH), F32),
            pltpu.VMEM((2, NKK, TOK, CH), F32),
            pltpu.VMEM((2, TOK, D), BF),
            pltpu.VMEM((128, 128), F32),
            pltpu.VMEM((2, 4, 2, 256, PAIR), BF),
            pltpu.SemaphoreType.DMA((140,)),
        ],
        compiler_params=pltpu.CompilerParams(
            collective_id=2, has_side_effects=True, vmem_limit_bytes=60 * 2 ** 20),
        name="give_back",
    )(forward, backward, x_fwd, x_bwd, cot, gain, metas)


def describe(routes, slots, logits):
    me = lax.axis_index("expert")
    core = lax.rem(me, 2)
    z = lax.rem(me // 2, 4)
    b = z // 2
    zl = lax.rem(z, 2)
    index = (b + zl - 2 * b * zl) * 2 + core
    affinity = jax.nn.sigmoid(logits)
    share = route_scale * affinity / jnp.sum(affinity, axis=-1, keepdims=True)
    key = (routes * PAIR + index * CAP + slots).astype(F32)
    table = jnp.concatenate([key.T, share.T, jnp.zeros((4, TOK), F32)], axis=0)
    zeros = jnp.zeros_like(table)
    return jnp.where(
        core == 0,
        jnp.concatenate([table, zeros], axis=1),
        jnp.concatenate([zeros, table], axis=1),
    )


def on_device(
    x_fwd, routes_fwd, slots_fwd, logits_fwd,
    x_bwd, cot_bwd, routes_bwd, slots_bwd, logits_bwd,
    gain, w_gate, w_up, w_down,
):
    meta = jnp.concatenate([
        describe(routes_fwd[0], slots_fwd[0], logits_fwd[0]),
        describe(routes_bwd[0], slots_bwd[0], logits_bwd[0]),
    ], axis=0)
    rows, metas = dispatch(x_fwd[0], x_bwd[0], cot_bwd[0], gain, meta)
    forward, backward = experts(rows, w_gate[0], w_up[0], w_down[0])
    arrived, returned = give_back(
        forward, backward, x_fwd[0], x_bwd[0], cot_bwd[0], gain, metas)
    return (arrived[None], returned[None])


def solution(mesh):
    return jax.shard_map(
        on_device,
        mesh=mesh,
        in_specs=(
            P("section", "expert", None),
            P("section", "expert", None),
            P("section", "expert", None),
            P("section", "expert", None),
            P("section", "expert", None),
            P("section", "expert", None),
            P("section", "expert", None),
            P("section", "expert", None),
            P("section", "expert", None),
            P("section", None),
            P("section", None, "expert"),
            P("section", None, "expert"),
            P("section", "expert", None),
        ),
        out_specs=(P("section", "expert", None), P("section", "expert", None)),
        check_vma=False,
    )
```

```python
import jax
import jax.numpy as jnp
from jax import lax
from jax.experimental import pallas as pl
from jax.experimental.pallas import tpu as pltpu
from jax.sharding import PartitionSpec as P

D = 7168
EXP_WIN = 4
TOPK = 2
CAP = 36
TOK = 64
HID = 512
PAIR = 4 * CAP
SLOTS = EXP_WIN * PAIR
CH = 896
NK = 4
NKK = 2 * NK

epsilon = 1e-06
route_scale = 2.5
MESH = pl.DeviceIdType.MESH
BF = jnp.bfloat16
F32 = jnp.float32


class Place:
    def __init__(self):
        me = lax.axis_index("expert")
        self.core = lax.rem(me, 2)
        z = lax.rem(me // 2, 4)
        a = me // 8
        b = z // 2
        zl = lax.rem(z, 2)
        self.h = b + zl - 2 * b * zl
        zg = z + 1 - 2 * zl

        def at(a_, z_, c_):
            return a_ * 8 + z_ * 2 + c_

        self.mate = at(a, z, 1 - self.core)
        self.g = at(a, zg, self.core)
        self.gmate = at(a, zg, 1 - self.core)
        self.c = at(a, 3 - z, self.core)
        self.y = at(1 - a, z, self.core)
        self.pairs = (a * 2 + b, a * 2 + 1 - b, (1 - a) * 2 + b, (1 - a) * 2 + 1 - b)
        self.me = me
        self.index = self.h * 2 + self.core


def coordinates(device, section=None):
    if section is None:
        return {"expert": device}
    return {"section": section, "expert": device}


class Copies:
    def __init__(self, sems):
        self.sems = sems
        self.used = 0

    def sem(self):
        self.used += 1
        return self.sems.at[self.used - 1]

    def remote(self, src, dst, device, section=None):
        copy = pltpu.make_async_remote_copy(
            src_ref=src,
            dst_ref=dst,
            send_sem=self.sem(),
            recv_sem=self.sem(),
            device_id=coordinates(device, section),
            device_id_type=MESH,
        )
        copy.start()
        return copy

    def local(self, src, dst):
        copy = pltpu.make_async_copy(src, dst, self.sem())
        copy.start()
        return copy


def greet(places):
    barrier = pltpu.get_barrier_semaphore()
    for place, section in places:
        pl.semaphore_signal(
            barrier, inc=1, device_id=coordinates(place, section), device_id_type=MESH)
    pl.semaphore_wait(barrier, len(places))


def rows64(first):
    return pl.ds(pl.multiple_of(first, 64), 64)


def rows128(first):
    return pl.ds(pl.multiple_of(first, 128), 128)


def rows144(pair):
    return pl.ds(pl.multiple_of(pair * PAIR, PAIR), PAIR)


CONTRACT = (((1,), (1,)), ((), ()))


def dot(a, b):
    return jnp.dot(a, b, preferred_element_type=F32)


def dot_t(a, b):
    return lax.dot_general(a, b, CONTRACT, preferred_element_type=F32)


class Experts:
    def __init__(self, cp, rows, wg, wu, wd, buffers, gate, up, dact, act, dg, du):
        self.cp = cp
        self.rows = rows
        self.wg, self.wu, self.wd = wg, wu, wd
        self.buffers = buffers
        self.gate, self.up, self.dact = gate, up, dact
        self.act, self.dg, self.du = act, dg, du
        self.jobs = []
        self.next = 0
        self.fetched = {}

    def plan(self, kind, t, kk):
        self.jobs.append((kind, t, kk))

    def fetch(self, j, early):
        if j >= len(self.jobs) or j in self.fetched:
            return
        kind, t, kk = self.jobs[j]
        if early and kind != "out" and kind != self.jobs[j - 1][0]:
            return
        if early and kind != "out" and t != self.jobs[j - 1][1]:
            return
        slot = j % 2
        a, b, c, d = (buf.at[slot] for buf in self.buffers)
        cols = pl.ds(pl.multiple_of(kk * CH, CH), CH)
        pairs = []
        if kind == "hidden":
            pairs.append((self.rows.at[t, kk], a))
        if kind == "cot":
            pairs.append((self.rows.at[t, kk], a))
        if kind == "hidden" or (kind == "out" and t == 0):
            pairs.append((self.wg.at[cols, :], b))
            pairs.append((self.wu.at[cols, :], c))
        if kind == "cot" or (kind == "out" and t == 2):
            pairs.append((self.wd.at[:, cols], d))
        self.fetched[j] = [self.cp.local(x, y) for x, y in pairs]

    def run(self):
        j = self.next
        self.next += 1
        self.fetch(j, False)
        self.fetch(j + 1, True)
        for copy in self.fetched[j]:
            copy.wait()
        kind, t, kk = self.jobs[j]
        a, b, c, d = (buf.at[j % 2] for buf in self.buffers)
        if kind == "hidden":
            gate = dot(a[...], b[...])
            up = dot(a[...], c[...])
            if kk == 0:
                self.gate[...] = gate
                self.up[...] = up
            else:
                self.gate[...] += gate
                self.up[...] += up
            if t == 2 and kk == NKK - 1:
                g = self.gate[...]
                self.act[...] = (g * jax.nn.sigmoid(g) * self.up[...]).astype(BF)
        elif kind == "cot":
            dact = dot_t(a[...], d[...])
            if kk == 0:
                self.dact[...] = dact
            else:
                self.dact[...] += dact
            if kk == NKK - 1:
                g = self.gate[...]
                s = jax.nn.sigmoid(g)
                v = self.dact[...]
                self.dg[...] = (v * self.up[...] * s * (1.0 + g * (1.0 - s))).astype(BF)
                self.du[...] = (v * g * s).astype(BF)
        elif t == 0:
            return dot_t(self.dg[...], b[...]) + dot_t(self.du[...], c[...])
        else:
            return dot(self.act[...], d[...])


def relay_kernel(
    xf, xb, cot, gain, meta, wg, wu, wd, yf_out, dx_out, rows,
    xin, hbuf, x_pair, tok, stage, relay, metas, place_m, meta_t, weights,
    part, total, from_cf, from_g, pass_y, from_yc, comb_own, comb_out, comb_in,
    spread, acc, result_b, result_f, out_stage,
    buf_a, buf_b, buf_c, buf_d, gate, up, dact, act, dg, du, sems,
):
    at = Place()
    cp = Copies(sems)
    me_s = lax.axis_index("section")
    up_s = lax.rem(me_s + 1, 8)
    down_s = lax.rem(me_s + 7, 8)
    h, core = at.h, at.core
    half = core * NK
    other = (1 - core) * NK

    loads = [cp.local(src, xin.at[t]) for t, src in enumerate((xb, cot, xf))]
    greet(
        [(d, None) for d in (at.mate, at.g, at.gmate, at.c, at.y)]
        + [(d, s) for d in (at.me, at.mate) for s in (up_s, down_s)])

    mine = metas.at[at.index]
    meta_sends = [cp.remote(meta, mine, d) for d in (at.mate, at.g, at.gmate)]
    metas[at.index] = meta[...]

    my_rows = h * 128 + core * 64
    tok_in = []
    scale = {}
    for t in range(3):
        loads[t].wait()
        src = xin.at[t]
        if t != 1:
            square = jnp.zeros((TOK, 1), F32)
            for kk in range(NKK):
                v = src[:, kk * CH:(kk + 1) * CH].astype(F32)
                square = square + jnp.sum(v * v, axis=-1, keepdims=True)
            scale[t] = lax.rsqrt(square / D + epsilon)
        for kk in range(NKK):
            v = src[:, kk * CH:(kk + 1) * CH]
            if t != 1:
                v = (v.astype(F32) * scale[t] * gain[:, kk * CH:(kk + 1) * CH]).astype(BF)
            hbuf[t, kk] = v
        tok_in.append(cp.remote(
            hbuf.at[t, pl.ds(other, NK)], tok.at[t, :, rows64(my_rows), :], at.mate))
        for k in range(NK):
            tok[t, k, rows64(my_rows), :] = hbuf[t, half + k]
        if t == 0:
            tok_in[0].wait_recv()

        if t == 0:
            steps = [(t_, i) for t_ in range(3) for i in range(NK)]
            n = len(steps)
            tok_g = {}

            def send_tokens(s):
                if s >= n:
                    return
                t_, i = steps[s]
                if i == 0 and t_ > 0:
                    tok_in[t_].wait_recv()
                q = lax.rem(2 * (1 - h) + i, NK)
                piece = tok.at[t_, q, rows128(h * 128), :]
                tok_g[s] = cp.remote(piece, piece, at.g)

            for s in range(3):
                send_tokens(s)
    x_in = cp.remote(
        xin.at[2, :, pl.ds(pl.multiple_of((1 - core) * NK * CH, 128), NK * CH)],
        x_pair.at[rows64(core * 64), :], at.mate)
    x_own = cp.local(
        xin.at[2, :, pl.ds(pl.multiple_of(core * NK * CH, 128), NK * CH)],
        x_pair.at[rows64(core * 64), :])

    for m in meta_sends:
        m.wait_recv()
    for fb in (1, 0):
        for rel in range(4):
            first = at.pairs[rel] * PAIR
            ids = (lax.broadcasted_iota(jnp.int32, (PAIR, 128), 0) + first).astype(F32)
            for hh in range(2):
                m = metas[2 * hh] + metas[2 * hh + 1]
                k0 = m[fb * 8:fb * 8 + 1, :]
                k1 = m[fb * 8 + 1:fb * 8 + 2, :]
                hit = jnp.where(ids == k0, 1.0, 0.0) + jnp.where(ids == k1, 1.0, 0.0)
                place_m[fb, rel, :, hh * 128:(hh + 1) * 128] = hit.astype(BF)

    sent = {}
    moved = {}
    passed = {}
    mate_in = {0: [], 1: [], 2: []}

    def gather(s):
        t, i = steps[s]
        slot = s % 3
        if s >= 3:
            for key in [k for k in list(sent) if k[0] == s - 3]:
                sent[key].wait_send()
            moved[s - 3].wait()
        tok_g[s].wait_recv()
        q = lax.rem(2 * h + i, NK)
        fb = 0 if t == 2 else 1
        block = tok[t, q]
        order = (3, 2, 1, 0) if i < 2 else (2, 1, 0)
        for rel in order:
            stage[slot, rel] = dot(place_m[fb, rel], block).astype(BF)
            src = stage.at[slot, rel]
            target = rows.at[t, half + q, rows144(at.pairs[0]), :]
            if rel == 3:
                sent[s, 3] = cp.remote(src, relay.at[t, i], at.y)
            elif rel == 2:
                sent[s, 2] = cp.remote(src, target, at.y)
            elif rel == 1:
                sent[s, 1] = cp.remote(src, target, at.c)
            else:
                moved[s] = cp.local(src, target)
                sent[s, 0] = cp.remote(src, target, at.mate)
                mate_in[t].append(sent[s, 0])

    def to_mate(t, chunk_, pair):
        piece = rows.at[t, half + chunk_, rows144(pair), :]
        copy = cp.remote(piece, piece, at.mate)
        mate_in[t].append(copy)
        passed[len(passed)] = copy

    def relayed(s):
        return 0 <= s < n and steps[s][1] < 2

    def relay_first(s):
        if not relayed(s):
            return
        t, i = steps[s]
        sent[s, 3].wait_recv()
        passed["c", s] = cp.remote(
            relay.at[t, i], rows.at[t, half + 2 * h + i, rows144(at.pairs[2]), :], at.c)

    def relay_second(s):
        if not relayed(s):
            return
        t, i = steps[s]
        passed["c", s].wait_recv()
        piece = rows.at[t, half + 2 * h + i, rows144(at.pairs[3]), :]
        passed["g", s] = cp.remote(piece, piece, at.g)
        to_mate(t, 2 * h + i, at.pairs[3])

    def relay_last(s):
        if not relayed(s):
            return
        t, i = steps[s]
        passed["g", s].wait_recv()
        to_mate(t, 2 * (1 - h) + i, at.pairs[3])

    def pass_on(s):
        if not 0 <= s < n:
            return
        t, i = steps[s]
        q = lax.rem(2 * h + i, NK)
        sent[s, 2].wait_recv()
        to_mate(t, q, at.pairs[2])
        sent[s, 1].wait_recv()
        to_mate(t, q, at.pairs[1])

    def complete(t):
        for m in mate_in[t]:
            m.wait_recv()
        if t == 2:
            for s in range(n - 3, n):
                moved[s].wait()

    def chunk(i):
        return lax.rem(2 * (1 - h) + i, NK)

    jobs = Experts(cp, rows, wg, wu, wd, (buf_a, buf_b, buf_c, buf_d),
                   gate, up, dact, act, dg, du)
    for kk in range(NKK):
        jobs.plan("hidden", 0, kk)
    for kk in range(NKK):
        jobs.plan("cot", 1, kk)
    for i in range(NK):
        jobs.plan("out", 0, other + chunk(i))
        jobs.plan("out", 0, half + chunk(i))
    for kk in range(NKK):
        jobs.plan("hidden", 2, kk)
    for i in range(NK):
        jobs.plan("out", 2, other + chunk(i))
        jobs.plan("out", 2, half + chunk(i))

    back = {}
    from_y = {0: tok.at[0], 1: tok.at[2]}
    parts = {}

    def arrived_c(r, q):
        return tok.at[1, q, 0:PAIR, :] if r == 0 else from_cf.at[q]

    def arrived_y(r, q):
        return from_y[r].at[q, 0:PAIR, :]

    def piece(r, q, rel):
        return total.at[r, q, rows144(at.pairs[rel]), :]

    def send_y(r, i):
        back["y", r, i] = cp.remote(piece(r, chunk(i), 2), arrived_y(r, chunk(i)), at.y)

    def send_c(r, i):
        back["c", r, i] = cp.remote(piece(r, chunk(i), 1), arrived_c(r, chunk(i)), at.c)

    def add_up(r, i):
        q = chunk(i)
        number = r * NK + i
        if number >= 2:
            parts[number - 2].wait_send()
        out_stage[number % 2] = jobs.run().astype(BF)
        parts[number] = cp.remote(out_stage.at[number % 2], part.at[q], at.mate)
        v = jobs.run()
        parts[number].wait_recv()
        total[r, q] = (v + part[q].astype(F32)).astype(BF)
        if i < 2:
            back["g", r, i] = cp.remote(piece(r, q, 3), from_g.at[r, i], at.g)
            send_y(r, i)
            send_c(r, i)
        else:
            back["g", r, i - 2].wait_recv()
            pass_y[r, i - 2] = (
                total[r, q, rows144(at.pairs[3]), :].astype(F32) + from_g[r, i - 2].astype(F32)
            ).astype(BF)
            back["yg", r, i] = cp.remote(pass_y.at[r, i - 2], from_yc.at[r, i - 2, 0], at.c)

    def relay_back(r, i):
        back["yg", r, i].wait_recv()
        back["ygy", r, i] = cp.remote(from_yc.at[r, i - 2, 0], from_yc.at[r, i - 2, 1], at.y)

    def combine(r, i):
        q = chunk(i)
        fb = 1 - r
        back["y", r, i].wait_recv()
        back["c", r, i].wait_recv()
        terms = [
            (0, total[r, q, rows144(at.pairs[0]), :]),
            (1, arrived_c(r, q)[...]),
            (2, arrived_y(r, q)[...]),
        ]
        if i >= 2:
            back["ygy", r, i].wait_recv()
            terms.append((3, from_yc[r, i - 2, 1]))
        v = jnp.zeros((256, CH), F32)
        for rel, rr in terms:
            v = v + dot(weights[fb, rel, 0], rr)
            v = v + dot(weights[fb, rel, 1], rr)
        if r == 1:
            back["u", 0, i].wait_send()
        comb_own[q] = v[0:128]
        comb_out[q] = v[128:256].astype(BF)
        back["u", r, i] = cp.remote(comb_out.at[q], comb_in.at[r, q], at.g)

    def finish_backward(i):
        q = chunk(i)
        back["u", 0, (i + 2) % NK].wait_recv()
        v = comb_own[q] + comb_in[0, q].astype(F32)
        spread[q, 0] = v[0:64]
        spread[q, 1] = v[64:128]
        back["d", i] = cp.remote(spread.at[q, 1 - core], acc.at[half + q], at.mate)
        acc[half + q] = spread[q, core]

    def finalize_backward():
        for i in range(NK):
            back["d", i].wait_recv()
        along = jnp.zeros((TOK, 1), F32)
        for kk in range(NKK):
            cols = slice(kk * CH, (kk + 1) * CH)
            x = xin[0, :, cols].astype(F32)
            along = along + jnp.sum(x * (gain[:, cols] * acc[kk]), axis=-1, keepdims=True)
        inverse = scale[0]
        factor = inverse * inverse * inverse * (along / D)
        for kk in range(NKK):
            cols = slice(kk * CH, (kk + 1) * CH)
            x = xin[0, :, cols].astype(F32)
            v = xin[1, :, cols].astype(F32) + inverse * (gain[:, cols] * acc[kk]) - x * factor
            result_b[:, cols] = v.astype(BF)
        back["s"] = cp.remote(result_b, dx_out, at.me, down_s)

    def finish_forward(i):
        q = chunk(i)
        back["u", 1, (i + 2) % NK].wait_recv()
        cols = pl.ds(pl.multiple_of(q * CH, CH), CH)
        v = x_pair[:, cols].astype(F32) + (comb_own[q] + comb_in[1, q].astype(F32))
        result_f[q] = v.astype(BF)
        target = yf_out.at[:, pl.ds(pl.multiple_of((half + q) * CH, CH), CH)]
        back["own", i] = cp.remote(
            result_f.at[q, rows64(core * 64), :], target, at.me, up_s)
        back["mate", i] = cp.remote(
            result_f.at[q, rows64((1 - core) * 64), :], target, at.mate, up_s)

    def mixing_weights():
        meta_t[...] = jnp.zeros_like(meta_t)
        for w in range(2):
            hh = h if w == 0 else 1 - h
            meta_t[0:16, :] = metas[2 * hh] + metas[2 * hh + 1]
            m = jnp.transpose(meta_t[...])
            for fb in range(2):
                for rel in range(4):
                    first = at.pairs[rel] * PAIR
                    ids = (lax.broadcasted_iota(jnp.int32, (128, PAIR), 1) + first).astype(F32)
                    c = fb * 8
                    v = jnp.where(ids == m[:, c:c + 1], m[:, c + 2:c + 3], 0.0)
                    v = v + jnp.where(ids == m[:, c + 1:c + 2], m[:, c + 3:c + 4], 0.0)
                    high = v.astype(BF)
                    weights[fb, rel, 0, w * 128:(w + 1) * 128, :] = high
                    weights[fb, rel, 1, w * 128:(w + 1) * 128, :] = (v - high.astype(F32)).astype(BF)

    def run(count):
        for _ in range(count):
            jobs.run()

    for s in range(n + 3):
        send_tokens(s + 3)
        if s >= 3:
            tok_g[s - 3].wait_send()
        if s < n:
            gather(s)
        relay_first(s - 1)
        relay_second(s - 2)
        pass_on(s - 1)
        relay_last(s - 3)
        if s == 4:
            mixing_weights()
        if s == 6:
            complete(0)
        if s in (6, 7, 8, 9):
            run(2)
        if s == 10:
            complete(1)
        if s in (10, 11):
            run(4)
        if s == n:
            add_up(0, 0)
        if s == n + 1:
            add_up(0, 1)
    complete(2)
    add_up(0, 2)
    add_up(0, 3)
    run(2)
    relay_back(0, 2)
    send_c(0, 2)
    run(2)
    relay_back(0, 3)
    send_c(0, 3)
    send_y(0, 2)
    send_y(0, 3)
    run(4)
    combine(0, 0)
    add_up(1, 0)
    combine(0, 1)
    add_up(1, 1)
    add_up(1, 2)
    add_up(1, 3)
    combine(0, 2)
    combine(0, 3)
    for i in range(NK):
        finish_backward(i)
    relay_back(1, 2)
    send_c(1, 2)
    relay_back(1, 3)
    send_c(1, 3)
    send_y(1, 2)
    send_y(1, 3)
    finalize_backward()
    x_in.wait_recv()
    x_own.wait()
    combine(1, 0)
    combine(1, 1)
    combine(1, 2)
    finish_forward(2)
    combine(1, 3)
    finish_forward(3)
    finish_forward(0)
    finish_forward(1)

    for m in meta_sends + tok_in + [x_in] + list(passed.values()):
        m.wait_send()
    for (s, rel), m in sent.items():
        if s >= n - 3:
            m.wait_send()
    for number in (2 * NK - 2, 2 * NK - 1):
        parts[number].wait_send()
    for key, m in back.items():
        if not (key[0] == "u" and key[1] == 0):
            m.wait_send()
    back["s"].wait_recv()
    for i in range(NK):
        back["own", i].wait_recv()
        back["mate", i].wait_recv()


def relay(x_fwd, x_bwd, cot, gain, meta, wg, wu, wd):
    vmem = pl.BlockSpec(memory_space=pltpu.VMEM)
    hbm = pl.BlockSpec(memory_space=pl.ANY)
    arrived, returned, _ = pl.pallas_call(
        relay_kernel,
        out_shape=(
            jax.ShapeDtypeStruct((TOK, D), BF),
            jax.ShapeDtypeStruct((TOK, D), BF),
            jax.ShapeDtypeStruct((3, NKK, SLOTS, CH), BF),
        ),
        in_specs=[hbm, hbm, hbm, vmem, vmem, hbm, hbm, hbm],
        out_specs=(hbm, hbm, hbm),
        scratch_shapes=[
            pltpu.VMEM((3, TOK, D), BF),
            pltpu.VMEM((3, NKK, TOK, CH), BF),
            pltpu.VMEM((128, NK * CH), BF),
            pltpu.VMEM((3, NK, 256, CH), BF),
            pltpu.VMEM((3, 4, PAIR, CH), BF),
            pltpu.VMEM((3, 2, PAIR, CH), BF),
            pltpu.VMEM((4, 16, 128), F32),
            pltpu.VMEM((2, 4, PAIR, 256), BF),
            pltpu.VMEM((128, 128), F32),
            pltpu.VMEM((2, 4, 2, 256, PAIR), BF),
            pltpu.VMEM((NK, SLOTS, CH), BF),
            pltpu.VMEM((2, NK, SLOTS, CH), BF),
            pltpu.VMEM((NK, PAIR, CH), BF),
            pltpu.VMEM((2, 2, PAIR, CH), BF),
            pltpu.VMEM((2, 2, PAIR, CH), BF),
            pltpu.VMEM((2, 2, 2, PAIR, CH), BF),
            pltpu.VMEM((NK, 128, CH), F32),
            pltpu.VMEM((NK, 128, CH), BF),
            pltpu.VMEM((2, NK, 128, CH), BF),
            pltpu.VMEM((NK, 2, TOK, CH), F32),
            pltpu.VMEM((NKK, TOK, CH), F32),
            pltpu.VMEM((TOK, D), BF),
            pltpu.VMEM((NK, 128, CH), BF),
            pltpu.VMEM((2, SLOTS, CH), BF),
            pltpu.VMEM((2, SLOTS, CH), BF),
            pltpu.VMEM((2, CH, HID), BF),
            pltpu.VMEM((2, CH, HID), BF),
            pltpu.VMEM((2, HID, CH), BF),
            pltpu.VMEM((SLOTS, HID), F32),
            pltpu.VMEM((SLOTS, HID), F32),
            pltpu.VMEM((SLOTS, HID), F32),
            pltpu.VMEM((SLOTS, HID), BF),
            pltpu.VMEM((SLOTS, HID), BF),
            pltpu.VMEM((SLOTS, HID), BF),
            pltpu.SemaphoreType.DMA((480,)),
        ],
        compiler_params=pltpu.CompilerParams(
            collective_id=1, has_side_effects=True, vmem_limit_bytes=64 * 2 ** 20),
        name="relay",
    )(x_fwd, x_bwd, cot, gain, meta, wg, wu, wd)
    return arrived, returned


def describe(routes, slots, logits):
    me = lax.axis_index("expert")
    core = lax.rem(me, 2)
    z = lax.rem(me // 2, 4)
    b = z // 2
    zl = lax.rem(z, 2)
    index = (b + zl - 2 * b * zl) * 2 + core
    affinity = jax.nn.sigmoid(logits)
    share = route_scale * affinity / jnp.sum(affinity, axis=-1, keepdims=True)
    key = (routes * PAIR + index * CAP + slots).astype(F32)
    table = jnp.concatenate([key.T, share.T, jnp.zeros((4, TOK), F32)], axis=0)
    zeros = jnp.zeros_like(table)
    return jnp.where(
        core == 0,
        jnp.concatenate([table, zeros], axis=1),
        jnp.concatenate([zeros, table], axis=1),
    )


def on_device(
    x_fwd, routes_fwd, slots_fwd, logits_fwd,
    x_bwd, cot_bwd, routes_bwd, slots_bwd, logits_bwd,
    gain, w_gate, w_up, w_down,
):
    meta = jnp.concatenate([
        describe(routes_fwd[0], slots_fwd[0], logits_fwd[0]),
        describe(routes_bwd[0], slots_bwd[0], logits_bwd[0]),
    ], axis=0)
    arrived, returned = relay(
        x_fwd[0], x_bwd[0], cot_bwd[0], gain, meta, w_gate[0], w_up[0], w_down[0])
    return (arrived[None], returned[None])


def solution(mesh):
    return jax.shard_map(
        on_device,
        mesh=mesh,
        in_specs=(
            P("section", "expert", None),
            P("section", "expert", None),
            P("section", "expert", None),
            P("section", "expert", None),
            P("section", "expert", None),
            P("section", "expert", None),
            P("section", "expert", None),
            P("section", "expert", None),
            P("section", "expert", None),
            P("section", None),
            P("section", None, "expert"),
            P("section", None, "expert"),
            P("section", "expert", None),
        ),
        out_specs=(P("section", "expert", None), P("section", "expert", None)),
        check_vma=False,
    )
```

```python
import jax
import jax.numpy as jnp
from jax import lax
from jax.experimental import pallas as pl
from jax.experimental.pallas import tpu as pltpu
from jax.sharding import PartitionSpec as P

D = 7168
EXP_WIN = 4
TOPK = 2
CAP = 36
TOK = 64
HID = 512
PAIR = 4 * CAP
SLOTS = EXP_WIN * PAIR
CH = 896
NK = 4
NKK = 2 * NK

epsilon = 1e-06
route_scale = 2.5
MESH = pl.DeviceIdType.MESH
BF = jnp.bfloat16
F32 = jnp.float32


class Place:
    def __init__(self):
        me = lax.axis_index("expert")
        self.core = lax.rem(me, 2)
        z = lax.rem(me // 2, 4)
        a = me // 8
        b = z // 2
        zl = lax.rem(z, 2)
        self.h = b + zl - 2 * b * zl
        zg = z + 1 - 2 * zl

        def at(a_, z_, c_):
            return a_ * 8 + z_ * 2 + c_

        self.mate = at(a, z, 1 - self.core)
        self.g = at(a, zg, self.core)
        self.gmate = at(a, zg, 1 - self.core)
        self.c = at(a, 3 - z, self.core)
        self.y = at(1 - a, z, self.core)
        self.ymate = at(1 - a, z, 1 - self.core)
        self.pairs = (a * 2 + b, a * 2 + 1 - b, (1 - a) * 2 + b, (1 - a) * 2 + 1 - b)
        self.me = me
        self.index = self.h * 2 + self.core


def coordinates(device, section=None):
    if section is None:
        return {"expert": device}
    return {"section": section, "expert": device}


class Copies:
    def __init__(self, sems):
        self.sems = sems
        self.used = 0

    def sem(self):
        self.used += 1
        return self.sems.at[self.used - 1]

    def remote(self, src, dst, device, section=None):
        copy = pltpu.make_async_remote_copy(
            src_ref=src,
            dst_ref=dst,
            send_sem=self.sem(),
            recv_sem=self.sem(),
            device_id=coordinates(device, section),
            device_id_type=MESH,
        )
        copy.start()
        return copy

    def local(self, src, dst):
        copy = pltpu.make_async_copy(src, dst, self.sem())
        copy.start()
        return copy


def rows64(first):
    return pl.ds(pl.multiple_of(first, 64), 64)


def rows128(first):
    return pl.ds(pl.multiple_of(first, 128), 128)


def rows144(pair):
    return pl.ds(pl.multiple_of(pair * PAIR, PAIR), PAIR)


CONTRACT = (((1,), (1,)), ((), ()))
ENDS = 600


def dot(a, b):
    return jnp.dot(a, b, preferred_element_type=F32)


def dot_t(a, b):
    return lax.dot_general(a, b, CONTRACT, preferred_element_type=F32)


class Experts:
    def __init__(self, cp, rows, wg, wu, wd, buffers, gate, up, dact, act, dg, du):
        self.cp = cp
        self.rows = rows
        self.wg, self.wu, self.wd = wg, wu, wd
        self.buffers = buffers
        self.gate, self.up, self.dact = gate, up, dact
        self.act, self.dg, self.du = act, dg, du
        self.jobs = []
        self.next = 0
        self.fetched = {}

    def plan(self, kind, t, kk):
        self.jobs.append((kind, t, kk))

    def fetch(self, j, early):
        if j >= len(self.jobs) or j in self.fetched:
            return
        kind, t, kk = self.jobs[j]
        if early and kind != "out" and kind != self.jobs[j - 1][0]:
            return
        if early and kind != "out" and t != self.jobs[j - 1][1]:
            return
        slot = j % 2
        a, b, c, d = (buf.at[slot] for buf in self.buffers)
        cols = pl.ds(pl.multiple_of(kk * CH, CH), CH)
        pairs = []
        if kind == "hidden":
            pairs.append((self.rows.at[t, kk], a))
        if kind == "cot":
            pairs.append((self.rows.at[t, kk], a))
        if kind == "hidden" or (kind == "out" and t == 0):
            pairs.append((self.wg.at[cols, :], b))
            pairs.append((self.wu.at[cols, :], c))
        if kind == "cot" or (kind == "out" and t == 2):
            pairs.append((self.wd.at[:, cols], d))
        self.fetched[j] = [self.cp.local(x, y) for x, y in pairs]

    def run(self):
        j = self.next
        self.next += 1
        self.fetch(j, False)
        self.fetch(j + 1, True)
        for copy in self.fetched[j]:
            copy.wait()
        kind, t, kk = self.jobs[j]
        a, b, c, d = (buf.at[j % 2] for buf in self.buffers)
        if kind == "hidden":
            gate = dot(a[...], b[...])
            up = dot(a[...], c[...])
            if kk == 0:
                self.gate[...] = gate
                self.up[...] = up
            else:
                self.gate[...] += gate
                self.up[...] += up
            if t == 2 and kk == NKK - 1:
                g = self.gate[...]
                self.act[...] = (g * jax.nn.sigmoid(g) * self.up[...]).astype(BF)
        elif kind == "cot":
            dact = dot_t(a[...], d[...])
            if kk == 0:
                self.dact[...] = dact
            else:
                self.dact[...] += dact
            if kk == NKK - 1:
                g = self.gate[...]
                s = jax.nn.sigmoid(g)
                v = self.dact[...]
                self.dg[...] = (v * self.up[...] * s * (1.0 + g * (1.0 - s))).astype(BF)
                self.du[...] = (v * g * s).astype(BF)
        elif t == 0:
            return dot_t(self.dg[...], b[...]) + dot_t(self.du[...], c[...])
        else:
            return dot(self.act[...], d[...])


def relay_kernel(
    xf, xb, cot, gain, routes_f, slots_f, logits_f, routes_b, slots_b, logits_b,
    wg, wu, wd, yf_parts, dx_out, rows,
    xin, hbuf, x_pair, tok, stage, relay, metas, place_m, meta_t, weights,
    part, total, from_cf, from_g, pass_y, from_yc, comb_own, comb_out, comb_in,
    spread, acc, both_own, both_in, out_stage,
    buf_a, buf_b, buf_c, buf_d, gate, up, dact, act, dg, du, sems,
):
    at = Place()
    cp = Copies(sems)
    me_s = lax.axis_index("section")
    up_s = lax.rem(me_s + 1, 8)
    down_s = lax.rem(me_s + 7, 8)
    up2_s = lax.rem(me_s + 2, 8)
    even = lax.rem(me_s, 2) == 0
    beside_s = me_s + 1 - 2 * lax.rem(me_s, 2)
    h, core = at.h, at.core
    half = core * NK
    other = (1 - core) * NK

    loads = [cp.local(src, xin.at[t]) for t, src in enumerate((xb, cot, xf))]
    friends = [(d, None) for d in (at.mate, at.g, at.gmate, at.c, at.y)]
    friends += [(d, s) for d in (at.me, at.mate, at.y, at.ymate) for s in (up_s, down_s)]
    friends += [(at.me, s) for s in (up2_s, lax.rem(me_s + 6, 8))]
    barrier = pltpu.get_barrier_semaphore()
    for place, section in friends:
        pl.semaphore_signal(
            barrier, inc=1, device_id=coordinates(place, section), device_id_type=MESH)
    lanes = lax.broadcasted_iota(jnp.int32, (TOPK, 128), 1) // TOK
    metas[0, at.index] = jnp.zeros((16, 128), F32)
    for fb, (routes, slots, logits) in enumerate(
            ((routes_f, slots_f, logits_f), (routes_b, slots_b, logits_b))):
        key = (routes[...] * PAIR + at.index * CAP + slots[...]).astype(F32)
        affinity = jax.nn.sigmoid(logits[...])
        share = route_scale * affinity / jnp.sum(affinity, axis=0, keepdims=True)
        for row, v in ((0, key), (TOPK, share)):
            v = jnp.where(lanes == core, jnp.concatenate([v, v], axis=1), 0.0)
            metas[0, at.index, fb * 8 + row:fb * 8 + row + TOPK, :] = v

    my_rows = h * 128 + core * 64
    tok_in = []
    scale = {}
    steps = [(t_, i) for t_ in range(3) for i in range(NK)]
    n = len(steps)
    tok_g = {}

    def send_tokens(s):
        if s >= n:
            return
        t_, i = steps[s]
        q = lax.rem(2 * (1 - h) + i, NK)
        target = tok.at[t_, q, rows64(my_rows), :]
        tok_g[s] = [
            cp.remote(hbuf.at[t_, half + q], target, at.g),
            cp.remote(hbuf.at[t_, other + q], target, at.gmate),
        ]

    for t in range(3):
        loads[t].wait()
        src = xin.at[t]
        if t != 1:
            square = jnp.zeros((TOK, 1), F32)
            for kk in range(NKK):
                v = src[:, kk * CH:(kk + 1) * CH].astype(F32)
                square = square + jnp.sum(v * v, axis=-1, keepdims=True)
            scale[t] = lax.rsqrt(square / D + epsilon)
        for kk in range(NKK):
            v = src[:, kk * CH:(kk + 1) * CH]
            if t != 1:
                v = (v.astype(F32) * scale[t] * gain[:, kk * CH:(kk + 1) * CH]).astype(BF)
            hbuf[t, kk] = v
        if t == 0:
            pl.semaphore_wait(barrier, len(friends))
            send_tokens(0)
        tok_in.append(cp.remote(
            hbuf.at[t, pl.ds(other, NK)], tok.at[t, :, rows64(my_rows), :], at.mate))
        if t == 0:
            mine = metas.at[0, at.index]
            meta_sends = [cp.remote(mine, mine, d) for d in (at.mate, at.g, at.gmate)]
        for k in range(NK):
            tok[t, k, rows64(my_rows), :] = hbuf[t, half + k]
    x_in = cp.remote(
        xin.at[2, :, pl.ds(pl.multiple_of((1 - core) * NK * CH, 128), NK * CH)],
        x_pair.at[rows64(core * 64), :], at.mate)
    x_own = cp.local(
        xin.at[2, :, pl.ds(pl.multiple_of(core * NK * CH, 128), NK * CH)],
        x_pair.at[rows64(core * 64), :])

    for m in meta_sends:
        m.wait_recv()
    meta_y = cp.remote(metas.at[0], metas.at[1], at.y)
    for fb in (1, 0):
        for rel in range(4):
            first = at.pairs[rel] * PAIR
            ids = (lax.broadcasted_iota(jnp.int32, (PAIR, 128), 0) + first).astype(F32)
            for hh in range(2):
                m = metas[0, 2 * hh] + metas[0, 2 * hh + 1]
                k0 = m[fb * 8:fb * 8 + 1, :]
                k1 = m[fb * 8 + 1:fb * 8 + 2, :]
                hit = jnp.where(ids == k0, 1.0, 0.0) + jnp.where(ids == k1, 1.0, 0.0)
                place_m[fb, rel, :, hh * 128:(hh + 1) * 128] = hit.astype(BF)
        if fb == 1:
            send_tokens(1)

    def split(t, i, which):
        return t == 1 and i == which

    sent = {}
    moved = {}
    passed = {}
    mate_in = {0: [], 1: [], 2: []}

    def settle(s):
        if s in moved:
            moved.pop(s).wait()

    def gather(s):
        t, i = steps[s]
        slot = s % 3
        if s >= 3:
            for key in [k for k in list(sent) if k[0] == s - 3]:
                sent[key].wait_send()
            settle(s - 3)
        if i == 0:
            tok_in[t].wait_recv()
        for m in tok_g[s]:
            m.wait_recv()
        if s == 0:
            send_tokens(2)
        q = lax.rem(2 * h + i, NK)
        fb = 0 if t == 2 else 1
        block = tok[t, q]
        order = (3, 2, 1, 0) if i < 2 else (2, 1, 0)
        for rel in order:
            if rel == 1 and split(t, i, 3):
                continue
            stage[slot, rel] = dot(place_m[fb, rel], block).astype(BF)
            src = stage.at[slot, rel]
            target = rows.at[t, half + q, rows144(at.pairs[0]), :]
            if rel == 3:
                sent[s, 3] = cp.remote(src, relay.at[t, i], at.y)
            elif rel == 2:
                sent[s, 2] = cp.remote(src, target, at.y)
            elif rel == 1:
                sent[s, 1] = cp.remote(src, target, at.c)
            else:
                moved[s] = cp.local(src, target)
                sent[s, 0] = cp.remote(src, target, at.mate)
                mate_in[t].append(sent[s, 0])

    def to_mate(t, chunk_, pair):
        piece = rows.at[t, half + chunk_, rows144(pair), :]
        copy = cp.remote(piece, piece, at.mate)
        mate_in[t].append(copy)
        passed[len(passed)] = copy

    def relayed(s):
        return 0 <= s < n and steps[s][1] < 2

    def relay_first(s):
        if not relayed(s):
            return
        t, i = steps[s]
        sent[s, 3].wait_recv()
        passed["c", s] = cp.remote(
            relay.at[t, i], rows.at[t, half + 2 * h + i, rows144(at.pairs[2]), :], at.c)

    def relay_second(s):
        if not relayed(s):
            return
        t, i = steps[s]
        passed["c", s].wait_recv()
        piece = rows.at[t, half + 2 * h + i, rows144(at.pairs[3]), :]
        passed["g", s] = cp.remote(piece, piece, at.g)
        to_mate(t, 2 * h + i, at.pairs[3])

    def relay_last(s):
        if not relayed(s):
            return
        t, i = steps[s]
        passed["g", s].wait_recv()
        to_mate(t, 2 * (1 - h) + i, at.pairs[3])

    def pass_on(s):
        if not 0 <= s < n:
            return
        t, i = steps[s]
        q = lax.rem(2 * h + i, NK)
        sent[s, 2].wait_recv()
        to_mate(t, q, at.pairs[2])
        if split(t, i, 3):
            return
        sent[s, 1].wait_recv()
        to_mate(t, q, at.pairs[1])
        if split(t, i, 1):
            piece_ = rows.at[t, half + q, rows144(at.pairs[1]), :]
            passed["e", t] = cp.remote(piece_, piece_, at.g)

    def pass_extra(s):
        if not 0 <= s < n:
            return
        t, i = steps[s]
        if split(t, i, 1):
            passed["e", t].wait_recv()
            to_mate(t, lax.rem(2 * h + 3, NK), at.pairs[1])

    def complete(t):
        for m in mate_in[t]:
            m.wait_recv()
        for s in range(t * NK, (t + 1) * NK):
            settle(s)

    def chunk(i):
        return lax.rem(2 * (1 - h) + i, NK)

    jobs = Experts(cp, rows, wg, wu, wd, (buf_a, buf_b, buf_c, buf_d),
                   gate, up, dact, act, dg, du)
    for kk in range(NKK):
        jobs.plan("hidden", 0, kk)
    for kk in range(NKK):
        jobs.plan("cot", 1, kk)
    for i in range(NK):
        jobs.plan("out", 0, other + chunk(i))
        jobs.plan("out", 0, half + chunk(i))
    for kk in range(NKK):
        jobs.plan("hidden", 2, kk)
    for i in range(NK):
        jobs.plan("out", 2, other + i)
        jobs.plan("out", 2, half + i)

    back = {}
    parts = {}

    def piece(r, q, rel):
        return total.at[r, q, rows144(at.pairs[rel]), :]

    def from_y(q):
        return tok.at[0, q, 0:PAIR, :]

    def from_c(q):
        return tok.at[1, q, 0:PAIR, :]

    def send_y(i):
        q = chunk(i)
        back["y", i] = cp.remote(piece(0, q, 2), from_y(q), at.y)

    def send_c(i):
        q = chunk(i)
        back["c", i] = cp.remote(piece(0, q, 1), from_c(q), at.c)

    def add_cores(r, i, q):
        number = r * NK + i
        if number >= 2:
            parts[number - 2].wait_send()
        out_stage[number % 2] = jobs.run().astype(BF)
        parts[number] = cp.remote(out_stage.at[number % 2], part.at[q], at.mate)
        v = jobs.run()
        parts[number].wait_recv()
        total[r, q] = (v + part[q].astype(F32)).astype(BF)

    def add_backward(i):
        q = chunk(i)
        add_cores(0, i, q)
        if i < 2:
            back["g", i] = cp.remote(piece(0, q, 3), from_g.at[i], at.g)
            send_y(i)
            send_c(i)
        else:
            back["g", i - 2].wait_recv()
            pass_y[i - 2] = (
                total[0, q, rows144(at.pairs[3]), :].astype(F32) + from_g[i - 2].astype(F32)
            ).astype(BF)
            back["yg", i] = cp.remote(pass_y.at[i - 2], from_yc.at[i - 2, 0], at.c)

    def relay_back(i):
        back["yg", i].wait_recv()
        back["ygy", i] = cp.remote(from_yc.at[i - 2, 0], from_yc.at[i - 2, 1], at.y)

    def mix(terms):
        v = jnp.zeros((256, terms[0][2].shape[-1]), F32)
        for fb, rel, rr in terms:
            v = v + dot(weights[fb, rel, 0], rr)
            v = v + dot(weights[fb, rel, 1], rr)
        return v

    def combine_backward(i):
        q = chunk(i)
        back["y", i].wait_recv()
        back["c", i].wait_recv()
        terms = [
            (1, 0, total[0, q, rows144(at.pairs[0]), :]),
            (1, 1, from_c(q)[...]),
            (1, 2, from_y(q)[...]),
        ]
        if i >= 2:
            back["ygy", i].wait_recv()
            terms.append((1, 3, from_yc[i - 2, 1]))
        v = mix(terms)
        comb_own[q] = v[0:128]
        comb_out[q] = v[128:256].astype(BF)
        back["u", i] = cp.remote(comb_out.at[q], comb_in.at[q], at.g)

    def span(piece_):
        return slice(0, 512) if piece_ == 0 else slice(512, CH)

    def forward_c(i, side):
        return tok.at[2, i, 0:PAIR, :] if side == 0 else from_cf.at[i]

    def add_forward(i):
        add_cores(1, i, i)
        for p in range(2):
            for side in range(2):
                rows_ = rows144(at.pairs[1 + 2 * side])
                back["fc", i, p, side] = cp.remote(
                    total.at[1, i, rows_, span(p)], forward_c(i, side).at[:, span(p)], at.c)

    def combine_forward(i, p):
        for side in range(2):
            back["fc", i, p, side].wait_recv()
            v = mix([
                (0, 2 * side, total[1, i, rows144(at.pairs[2 * side]), span(p)]),
                (0, 2 * side + 1, forward_c(i, side)[:, span(p)]),
            ])
            both_own[i, side, :, span(p)] = v[0:128]
            m = 2 * i + side
            out = stage.at[m // 4, m % 4, 0:128, span(p)]
            out[...] = v[128:256].astype(BF)
            back["fu", i, p, side] = cp.remote(out, both_in.at[i, side, :, span(p)], at.g)

    def finish_forward(i, p):
        first = 0 if p == 0 else 512
        width = 512 if p == 0 else CH - 512
        for side in (1, 0):
            back["fu", i, p, side].wait_recv()
            v = both_own[i, side, :, span(p)] + both_in[i, side, :, span(p)].astype(F32)
            if side == 0:
                v = v + x_pair[:, i * CH + first:i * CH + first + width].astype(F32)
            v = v.astype(BF)
            target = yf_parts.at[
                2 * side, :, pl.ds(pl.multiple_of((half + i) * CH + first, 128), width)]
            to = (at.me, at.mate) if side == 0 else (at.y, at.ymate)
            section = up_s if side == 0 else beside_s
            for c in range(2):
                hbuf[side, 2 * i + c, :, span(p)] = v[c * 64:(c + 1) * 64]
            back["own", i, p, side] = cp.remote(
                hbuf.at[side, 2 * i + core, :, span(p)], target, to[0], section)
            back["mate", i, p, side] = cp.remote(
                hbuf.at[side, 2 * i + 1 - core, :, span(p)], target, to[1], section)

    def send_up(i, p):
        first = 0 if p == 0 else 512
        width = 512 if p == 0 else CH - 512
        ends = []
        for part_ in (half, other):
            cols = pl.ds(pl.multiple_of((part_ + i) * CH + first, 128), width)
            ends.append((cols, cp.sem(), cp.sem()))

        @pl.when(even)
        def _():
            for kind, (cols, send, recv) in zip(("own", "mate"), ends):
                back[kind, i, p, 1].wait_recv()
                pltpu.make_async_remote_copy(
                    src_ref=yf_parts.at[2, :, cols], dst_ref=yf_parts.at[1, :, cols],
                    send_sem=send, recv_sem=recv,
                    device_id=coordinates(at.me, up2_s), device_id_type=MESH,
                ).start()

        @pl.when(jnp.logical_not(even))
        def _():
            for kind in ("own", "mate"):
                back[kind, i, p, 1].wait_recv()

        return ends

    def wait_up(ends):
        @pl.when(even)
        def _():
            for cols, send, recv in ends:
                copy = pltpu.make_async_remote_copy(
                    src_ref=yf_parts.at[2, :, cols], dst_ref=yf_parts.at[1, :, cols],
                    send_sem=send, recv_sem=recv,
                    device_id=coordinates(at.me, up2_s), device_id_type=MESH,
                )
                copy.wait_send()
                copy.wait_recv()

    def finish_backward(i):
        q = chunk(i)
        back["u", (i + 2) % NK].wait_recv()
        v = comb_own[q] + comb_in[q].astype(F32)
        spread[q, 0] = v[0:64]
        spread[q, 1] = v[64:128]
        back["d", i] = cp.remote(spread.at[q, 1 - core], acc.at[half + q], at.mate)
        acc[half + q] = spread[q, core]

    def finalize_backward():
        for i in range(NK):
            back["d", i].wait_recv()
        along = jnp.zeros((TOK, 1), F32)
        for kk in range(NKK):
            cols = slice(kk * CH, (kk + 1) * CH)
            x = xin[0, :, cols].astype(F32)
            along = along + jnp.sum(x * (gain[:, cols] * acc[kk]), axis=-1, keepdims=True)
        inverse = scale[0]
        factor = inverse * inverse * inverse * (along / D)
        for kk in range(NKK):
            cols = slice(kk * CH, (kk + 1) * CH)
            x = xin[0, :, cols].astype(F32)
            v = xin[1, :, cols].astype(F32) + inverse * (gain[:, cols] * acc[kk]) - x * factor
            xin[2, :, cols] = v.astype(BF)
        back["s"] = cp.remote(xin.at[2], dx_out, at.me, down_s)

    def mixing_weights():
        meta_y.wait_recv()
        meta_t[...] = jnp.zeros_like(meta_t)
        for side in range(2):
            for w in range(2):
                hh = h if w == 0 else 1 - h
                meta_t[0:16, :] = metas[side, 2 * hh] + metas[side, 2 * hh + 1]
                m = jnp.transpose(meta_t[...])
                todo = [(0, 2 * side + rel, rel) for rel in range(2)]
                if side == 0:
                    todo = todo + [(1, rel, rel) for rel in range(4)]
                for fb, place, rel in todo:
                    first = at.pairs[rel] * PAIR
                    ids = (lax.broadcasted_iota(jnp.int32, (128, PAIR), 1) + first).astype(F32)
                    c = fb * 8
                    v = jnp.where(ids == m[:, c:c + 1], m[:, c + 2:c + 3], 0.0)
                    v = v + jnp.where(ids == m[:, c + 1:c + 2], m[:, c + 3:c + 4], 0.0)
                    high = v.astype(BF)
                    weights[fb, place, 0, w * 128:(w + 1) * 128, :] = high
                    weights[fb, place, 1, w * 128:(w + 1) * 128, :] = (
                        v - high.astype(F32)).astype(BF)

    def run(count):
        for _ in range(count):
            jobs.run()

    for s in range(n + 3):
        if s > 0:
            send_tokens(s + 2)
        if s >= 3:
            for m in tok_g[s - 3]:
                m.wait_send()
        if s < n:
            gather(s)
        relay_first(s - 1)
        if s == n - 1:
            add_backward(0)
        relay_second(s - 2)
        pass_on(s - 2)
        if s >= n:
            add_backward(s - 11)
        relay_last(s - 3)
        pass_extra(s - 4)
        if s == 4:
            mixing_weights()
        if s == 6:
            complete(0)
        if s in (6, 7):
            run(3)
        if s == 8:
            run(2)
        if s == 9:
            complete(1)
        if s in (9, 10):
            run(4)
    complete(2)
    send_c(2)
    send_y(2)
    send_c(3)
    send_y(3)
    run(3)
    relay_back(2)
    combine_backward(0)
    run(3)
    relay_back(3)
    combine_backward(1)
    run(2)
    for (s, rel), m in sent.items():
        if s >= n - 3:
            m.wait_send()
    for m in tok_in + [x_in]:
        m.wait_send()
    x_in.wait_recv()
    x_own.wait()
    add_forward(0)
    combine_backward(2)
    add_forward(1)
    combine_backward(3)
    finish_backward(2)
    finish_backward(3)
    combine_forward(0, 0)
    add_forward(2)
    finish_backward(0)
    finish_backward(1)
    combine_forward(0, 1)
    finalize_backward()
    add_forward(3)
    gone = []
    combine_forward(1, 0)
    finish_forward(0, 0)
    combine_forward(1, 1)
    finish_forward(0, 1)
    gone.append(send_up(0, 0))
    combine_forward(2, 0)
    finish_forward(1, 0)
    gone.append(send_up(0, 1))
    combine_forward(2, 1)
    finish_forward(1, 1)
    gone.append(send_up(1, 0))
    combine_forward(3, 0)
    finish_forward(2, 0)
    gone.append(send_up(1, 1))
    combine_forward(3, 1)
    finish_forward(2, 1)
    gone.append(send_up(2, 0))
    finish_forward(3, 0)
    gone.append(send_up(2, 1))
    finish_forward(3, 1)
    gone.append(send_up(3, 0))
    gone.append(send_up(3, 1))

    assert cp.used <= ENDS, cp.used
    for m in meta_sends + [meta_y] + list(passed.values()):
        m.wait_send()
    for number in (2 * NK - 2, 2 * NK - 1):
        parts[number].wait_send()
    for m in back.values():
        m.wait_send()
    back["s"].wait_recv()
    for key, m in back.items():
        if key[0] in ("own", "mate") and key[3] == 0:
            m.wait_recv()
    for ends in gone:
        wait_up(ends)


def relay(x_fwd, x_bwd, cot, gain, tables, wg, wu, wd):
    vmem = pl.BlockSpec(memory_space=pltpu.VMEM)
    hbm = pl.BlockSpec(memory_space=pl.ANY)
    arrived_parts, returned, _ = pl.pallas_call(
        relay_kernel,
        out_shape=(
            jax.ShapeDtypeStruct((3, TOK, D), BF),
            jax.ShapeDtypeStruct((TOK, D), BF),
            jax.ShapeDtypeStruct((3, NKK, SLOTS, CH), BF),
        ),
        in_specs=[hbm] * 3 + [vmem] * 7 + [hbm] * 3,
        out_specs=(hbm, hbm, hbm),
        scratch_shapes=[
            pltpu.VMEM((3, TOK, D), BF),
            pltpu.VMEM((3, NKK, TOK, CH), BF),
            pltpu.VMEM((128, NK * CH), BF),
            pltpu.VMEM((3, NK, 256, CH), BF),
            pltpu.VMEM((3, 4, PAIR, CH), BF),
            pltpu.VMEM((3, 2, PAIR, CH), BF),
            pltpu.VMEM((2, 4, 16, 128), F32),
            pltpu.VMEM((2, 4, PAIR, 256), BF),
            pltpu.VMEM((128, 128), F32),
            pltpu.VMEM((2, 4, 2, 256, PAIR), BF),
            pltpu.VMEM((NK, SLOTS, CH), BF),
            pltpu.VMEM((2, NK, SLOTS, CH), BF),
            pltpu.VMEM((NK, PAIR, CH), BF),
            pltpu.VMEM((2, PAIR, CH), BF),
            pltpu.VMEM((2, PAIR, CH), BF),
            pltpu.VMEM((2, 2, PAIR, CH), BF),
            pltpu.VMEM((NK, 128, CH), F32),
            pltpu.VMEM((NK, 128, CH), BF),
            pltpu.VMEM((NK, 128, CH), BF),
            pltpu.VMEM((NK, 2, TOK, CH), F32),
            pltpu.VMEM((NKK, TOK, CH), F32),
            pltpu.VMEM((NK, 2, 128, CH), F32),
            pltpu.VMEM((NK, 2, 128, CH), BF),
            pltpu.VMEM((2, SLOTS, CH), BF),
            pltpu.VMEM((2, SLOTS, CH), BF),
            pltpu.VMEM((2, CH, HID), BF),
            pltpu.VMEM((2, CH, HID), BF),
            pltpu.VMEM((2, HID, CH), BF),
            pltpu.VMEM((SLOTS, HID), F32),
            pltpu.VMEM((SLOTS, HID), F32),
            pltpu.VMEM((SLOTS, HID), F32),
            pltpu.VMEM((SLOTS, HID), BF),
            pltpu.VMEM((SLOTS, HID), BF),
            pltpu.VMEM((SLOTS, HID), BF),
            pltpu.SemaphoreType.DMA((ENDS,)),
        ],
        compiler_params=pltpu.CompilerParams(
            collective_id=1, has_side_effects=True, vmem_limit_bytes=64 * 2 ** 20),
        name="relay",
    )(x_fwd, x_bwd, cot, gain, *tables, wg, wu, wd)
    odd = lax.rem(lax.axis_index("section"), 2) == 1
    across = jnp.where(odd, arrived_parts[2], arrived_parts[1])
    arrived = arrived_parts[0].astype(F32) + across.astype(F32)
    return arrived.astype(BF), returned


def on_device(
    x_fwd, routes_fwd, slots_fwd, logits_fwd,
    x_bwd, cot_bwd, routes_bwd, slots_bwd, logits_bwd,
    gain, w_gate, w_up, w_down,
):
    tables = [
        v[0].T for v in (
            routes_fwd, slots_fwd, logits_fwd, routes_bwd, slots_bwd, logits_bwd)
    ]
    arrived, returned = relay(
        x_fwd[0], x_bwd[0], cot_bwd[0], gain, tables, w_gate[0], w_up[0], w_down[0])
    return (arrived[None], returned[None])


def solution(mesh):
    return jax.shard_map(
        on_device,
        mesh=mesh,
        in_specs=(
            P("section", "expert", None),
            P("section", "expert", None),
            P("section", "expert", None),
            P("section", "expert", None),
            P("section", "expert", None),
            P("section", "expert", None),
            P("section", "expert", None),
            P("section", "expert", None),
            P("section", "expert", None),
            P("section", None),
            P("section", None, "expert"),
            P("section", None, "expert"),
            P("section", "expert", None),
        ),
        out_specs=(P("section", "expert", None), P("section", "expert", None)),
        check_vma=False,
    )
```

```python
import jax
import jax.numpy as jnp
from jax import lax
from jax.experimental import pallas as pl
from jax.experimental.pallas import tpu as pltpu
from jax.sharding import PartitionSpec as P

D = 7168
EXP_WIN = 4
TOPK = 2
CAP = 36
TOK = 64
HID = 512
PAIR = 4 * CAP
SLOTS = EXP_WIN * PAIR
CH = 896
NK = 4
NKK = 2 * NK

epsilon = 1e-06
route_scale = 2.5
MESH = pl.DeviceIdType.MESH
BF = jnp.bfloat16
F32 = jnp.float32


class Place:
    def __init__(self):
        me = lax.axis_index("expert")
        self.core = lax.rem(me, 2)
        z = lax.rem(me // 2, 4)
        a = me // 8
        b = z // 2
        zl = lax.rem(z, 2)
        self.h = b + zl - 2 * b * zl
        zg = z + 1 - 2 * zl

        def at(a_, z_, c_):
            return a_ * 8 + z_ * 2 + c_

        self.mate = at(a, z, 1 - self.core)
        self.g = at(a, zg, self.core)
        self.gmate = at(a, zg, 1 - self.core)
        self.c = at(a, 3 - z, self.core)
        self.y = at(1 - a, z, self.core)
        self.ymate = at(1 - a, z, 1 - self.core)
        self.pairs = (a * 2 + b, a * 2 + 1 - b, (1 - a) * 2 + b, (1 - a) * 2 + 1 - b)
        self.me = me
        self.index = self.h * 2 + self.core


def coordinates(device, section=None):
    if section is None:
        return {"expert": device}
    return {"section": section, "expert": device}


class Copies:
    def __init__(self, sems):
        self.sems = sems
        self.used = 0

    def sem(self):
        self.used += 1
        return self.sems.at[self.used - 1]

    def remote(self, src, dst, device, section=None):
        copy = pltpu.make_async_remote_copy(
            src_ref=src,
            dst_ref=dst,
            send_sem=self.sem(),
            recv_sem=self.sem(),
            device_id=coordinates(device, section),
            device_id_type=MESH,
        )
        copy.start()
        return copy

    def local(self, src, dst):
        copy = pltpu.make_async_copy(src, dst, self.sem())
        copy.start()
        return copy


def rows64(first):
    return pl.ds(pl.multiple_of(first, 64), 64)


def rows128(first):
    return pl.ds(pl.multiple_of(first, 128), 128)


def rows144(pair):
    return pl.ds(pl.multiple_of(pair * PAIR, PAIR), PAIR)


CONTRACT = (((1,), (1,)), ((), ()))
ENDS = 640


def dot(a, b):
    return jnp.dot(a, b, preferred_element_type=F32)


def dot_t(a, b):
    return lax.dot_general(a, b, CONTRACT, preferred_element_type=F32)


class Group:
    def __init__(self, copies):
        self.copies = copies

    def wait(self):
        for copy in self.copies:
            copy.wait()

    def wait_send(self):
        for copy in self.copies:
            copy.wait_send()

    def wait_recv(self):
        for copy in self.copies:
            copy.wait_recv()


class Experts:
    def __init__(self, cp, rows, wg, wu, wd, buffers, gate, up, dact, act, dg, du):
        self.cp = cp
        self.rows = rows
        self.wg, self.wu, self.wd = wg, wu, wd
        self.buffers = buffers
        self.gate, self.up, self.dact = gate, up, dact
        self.act, self.dg, self.du = act, dg, du
        self.jobs = []
        self.next = 0
        self.fetched = {}

    def plan(self, kind, t, kk):
        self.jobs.append((kind, t, kk))

    def fetch(self, j, early):
        if j >= len(self.jobs) or j in self.fetched:
            return
        kind, t, kk = self.jobs[j]
        if early and kind != "out" and kind != self.jobs[j - 1][0]:
            return
        if early and kind != "out" and t != self.jobs[j - 1][1]:
            return
        slot = j % 2
        a, b, c, d = (buf.at[slot] for buf in self.buffers)
        cols = pl.ds(pl.multiple_of(kk * CH, CH), CH)
        pairs = []
        if kind == "hidden":
            pairs.append((self.rows.at[t, kk], a))
        if kind == "cot":
            pairs.append((self.rows.at[t, kk], a))
        if kind == "hidden" or (kind == "out" and t == 0):
            pairs.append((self.wg.at[cols, :], b))
            pairs.append((self.wu.at[cols, :], c))
        if kind == "cot" or (kind == "out" and t == 2):
            pairs.append((self.wd.at[:, cols], d))
        self.fetched[j] = [self.cp.local(x, y) for x, y in pairs]

    def run(self):
        j = self.next
        self.next += 1
        self.fetch(j, False)
        self.fetch(j + 1, True)
        for copy in self.fetched[j]:
            copy.wait()
        kind, t, kk = self.jobs[j]
        a, b, c, d = (buf.at[j % 2] for buf in self.buffers)
        if kind == "hidden":
            gate = dot(a[...], b[...])
            up = dot(a[...], c[...])
            if kk == 0:
                self.gate[...] = gate
                self.up[...] = up
            else:
                self.gate[...] += gate
                self.up[...] += up
            if t == 2 and kk == NKK - 1:
                g = self.gate[...]
                self.act[...] = (g * jax.nn.sigmoid(g) * self.up[...]).astype(BF)
        elif kind == "cot":
            dact = dot_t(a[...], d[...])
            if kk == 0:
                self.dact[...] = dact
            else:
                self.dact[...] += dact
            if kk == NKK - 1:
                g = self.gate[...]
                s = jax.nn.sigmoid(g)
                v = self.dact[...]
                self.dg[...] = (v * self.up[...] * s * (1.0 + g * (1.0 - s))).astype(BF)
                self.du[...] = (v * g * s).astype(BF)
        elif t == 0:
            return dot_t(self.dg[...], b[...]) + dot_t(self.du[...], c[...])
        else:
            return dot(self.act[...], d[...])


def relay_kernel(
    xf, xb, cot, gain, routes_f, slots_f, logits_f, routes_b, slots_b, logits_b,
    wg, wu, wd, yf_parts, dx_out, rows,
    xin, hbuf, x_pair, tok, stage, relay, metas, place_m, meta_t, weights,
    part, total, from_cf, from_g, pass_y, from_yc, comb_own, comb_out, comb_in,
    spread, acc, both_own, both_in, out_stage,
    buf_a, buf_b, buf_c, buf_d, gate, up, dact, act, dg, du, sems,
):
    at = Place()
    cp = Copies(sems)
    me_s = lax.axis_index("section")
    up_s = lax.rem(me_s + 1, 8)
    down_s = lax.rem(me_s + 7, 8)
    up2_s = lax.rem(me_s + 2, 8)
    even = lax.rem(me_s, 2) == 0
    beside_s = me_s + 1 - 2 * lax.rem(me_s, 2)
    h, core = at.h, at.core
    half = core * NK
    other = (1 - core) * NK

    loads = [cp.local(src, xin.at[t]) for t, src in enumerate((xb, cot, xf))]
    friends = [(d, None) for d in (at.mate, at.g, at.gmate, at.c, at.y)]
    friends += [(d, s) for d in (at.me, at.mate, at.y, at.ymate) for s in (up_s, down_s)]
    friends += [(at.me, s) for s in (up2_s, lax.rem(me_s + 6, 8))]
    barrier = pltpu.get_barrier_semaphore()
    for place, section in friends:
        pl.semaphore_signal(
            barrier, inc=1, device_id=coordinates(place, section), device_id_type=MESH)
    lanes = lax.broadcasted_iota(jnp.int32, (TOPK, 128), 1) // TOK
    metas[0, at.index] = jnp.zeros((16, 128), F32)
    for fb, (routes, slots, logits) in enumerate(
            ((routes_f, slots_f, logits_f), (routes_b, slots_b, logits_b))):
        key = (routes[...] * PAIR + at.index * CAP + slots[...]).astype(F32)
        affinity = jax.nn.sigmoid(logits[...])
        share = route_scale * affinity / jnp.sum(affinity, axis=0, keepdims=True)
        for row, v in ((0, key), (TOPK, share)):
            v = jnp.where(lanes == core, jnp.concatenate([v, v], axis=1), 0.0)
            metas[0, at.index, fb * 8 + row:fb * 8 + row + TOPK, :] = v

    my_rows = h * 128 + core * 64
    tok_in = []
    scale = {}
    steps = [(t_, i) for t_ in range(3) for i in range(NK)]
    n = len(steps)
    tok_g = {}

    def pieces(s):
        return (slice(0, 512), slice(512, CH)) if s == 0 else (slice(0, CH),)

    def send_tokens(s):
        if s >= n:
            return
        t_, i = steps[s]
        q = lax.rem(2 * (1 - h) + i, NK)
        tok_g[s] = []
        for cols in pieces(s):
            target = tok.at[t_, q, rows64(my_rows), cols]
            tok_g[s].append(Group([
                cp.remote(hbuf.at[t_, half + q, :, cols], target, at.g),
                cp.remote(hbuf.at[t_, other + q, :, cols], target, at.gmate),
            ]))

    for t in range(3):
        loads[t].wait()
        src = xin.at[t]
        if t != 1:
            square = jnp.zeros((TOK, 1), F32)
            for kk in range(NKK):
                v = src[:, kk * CH:(kk + 1) * CH].astype(F32)
                square = square + jnp.sum(v * v, axis=-1, keepdims=True)
            scale[t] = lax.rsqrt(square / D + epsilon)
        for kk in range(NKK):
            v = src[:, kk * CH:(kk + 1) * CH]
            if t != 1:
                v = (v.astype(F32) * scale[t] * gain[:, kk * CH:(kk + 1) * CH]).astype(BF)
            hbuf[t, kk] = v
        if t == 0:
            pl.semaphore_wait(barrier, len(friends))
            mine = metas.at[0, at.index]
            meta_sends = [cp.remote(mine, mine, d) for d in (at.mate, at.g, at.gmate)]
            send_tokens(0)
        tok_in.append(cp.remote(
            hbuf.at[t, pl.ds(other, NK)], tok.at[t, :, rows64(my_rows), :], at.mate))
        for k in range(NK):
            tok[t, k, rows64(my_rows), :] = hbuf[t, half + k]
    x_in = cp.remote(
        xin.at[2, :, pl.ds(pl.multiple_of((1 - core) * NK * CH, 128), NK * CH)],
        x_pair.at[rows64(core * 64), :], at.mate)
    x_own = cp.local(
        xin.at[2, :, pl.ds(pl.multiple_of(core * NK * CH, 128), NK * CH)],
        x_pair.at[rows64(core * 64), :])

    for m in meta_sends:
        m.wait_recv()
    meta_y = cp.remote(metas.at[0], metas.at[1], at.y)
    def placing(fb):
        for rel in (3, 2, 1, 0):
            first = at.pairs[rel] * PAIR
            ids = (lax.broadcasted_iota(jnp.int32, (PAIR, 128), 0) + first).astype(F32)
            for hh in range(2):
                m = metas[0, 2 * hh] + metas[0, 2 * hh + 1]
                k0 = m[fb * 8:fb * 8 + 1, :]
                k1 = m[fb * 8 + 1:fb * 8 + 2, :]
                hit = jnp.where((ids == k0) | (ids == k1), 1.0, 0.0)
                place_m[fb, rel, :, hh * 128:(hh + 1) * 128] = hit.astype(BF)

    placing(1)
    send_tokens(1)

    def split(t, i, which):
        return t == 1 and i == which

    sent = {}
    moved = {}
    passed = {}
    mate_in = {0: [], 1: [], 2: []}

    def settle(s):
        if s in moved:
            moved.pop(s).wait()

    def gather(s):
        t, i = steps[s]
        slot = s % 3
        if s >= 3:
            for key in [k for k in list(sent) if k[0] == s - 3]:
                sent[key].wait_send()
            settle(s - 3)
        if i == 0:
            tok_in[t].wait_recv()
        q = lax.rem(2 * h + i, NK)
        fb = 0 if t == 2 else 1
        order = [rel for rel in (3, 2, 1, 0)
                 if not (rel == 3 and i >= 2) and not (rel == 1 and split(t, i, 3))]
        copies = {rel: [] for rel in order}
        local = []
        for cols, arrival in zip(pieces(s), tok_g[s]):
            arrival.wait_recv()
            block = tok[t, q, :, cols]
            for rel in order:
                stage[slot, rel, :, cols] = dot(place_m[fb, rel], block).astype(BF)
                src = stage.at[slot, rel, :, cols]
                target = rows.at[t, half + q, rows144(at.pairs[0]), cols]
                if rel == 3:
                    copies[3].append(cp.remote(src, relay.at[t, i, :, cols], at.y))
                elif rel == 2:
                    copies[2].append(cp.remote(src, target, at.y))
                elif rel == 1:
                    copies[1].append(cp.remote(src, target, at.c))
                else:
                    local.append(cp.local(src, target))
                    copies[0].append(cp.remote(src, target, at.mate))
        if s == 0:
            send_tokens(2)
        moved[s] = Group(local)
        for rel in order:
            sent[s, rel] = Group(copies[rel])
        mate_in[t].append(sent[s, 0])

    def to_mate(t, chunk_, pair):
        piece = rows.at[t, half + chunk_, rows144(pair), :]
        copy = cp.remote(piece, piece, at.mate)
        mate_in[t].append(copy)
        passed[len(passed)] = copy

    def relayed(s):
        return 0 <= s < n and steps[s][1] < 2

    def relay_first(s):
        if not relayed(s):
            return
        t, i = steps[s]
        sent[s, 3].wait_recv()
        passed["c", s] = cp.remote(
            relay.at[t, i], rows.at[t, half + 2 * h + i, rows144(at.pairs[2]), :], at.c)

    def relay_second(s):
        if not relayed(s):
            return
        t, i = steps[s]
        passed["c", s].wait_recv()
        piece = rows.at[t, half + 2 * h + i, rows144(at.pairs[3]), :]
        passed["g", s] = cp.remote(piece, piece, at.g)
        to_mate(t, 2 * h + i, at.pairs[3])

    def relay_last(s):
        if not relayed(s):
            return
        t, i = steps[s]
        passed["g", s].wait_recv()
        to_mate(t, 2 * (1 - h) + i, at.pairs[3])

    def pass_on(s):
        if not 0 <= s < n:
            return
        t, i = steps[s]
        q = lax.rem(2 * h + i, NK)
        sent[s, 2].wait_recv()
        to_mate(t, q, at.pairs[2])
        if split(t, i, 3):
            return
        sent[s, 1].wait_recv()
        to_mate(t, q, at.pairs[1])
        if split(t, i, 1):
            piece_ = rows.at[t, half + q, rows144(at.pairs[1]), :]
            passed["e", t] = cp.remote(piece_, piece_, at.g)

    def pass_extra(s):
        if not 0 <= s < n:
            return
        t, i = steps[s]
        if split(t, i, 1):
            passed["e", t].wait_recv()
            to_mate(t, lax.rem(2 * h + 3, NK), at.pairs[1])

    def complete(t):
        for m in mate_in[t]:
            m.wait_recv()
        for s in range(t * NK, (t + 1) * NK):
            settle(s)

    def chunk(i):
        return lax.rem(2 * (1 - h) + i, NK)

    jobs = Experts(cp, rows, wg, wu, wd, (buf_a, buf_b, buf_c, buf_d),
                   gate, up, dact, act, dg, du)
    for kk in range(NKK):
        jobs.plan("hidden", 0, kk)
    for kk in range(NKK):
        jobs.plan("cot", 1, kk)
    for i in range(NK):
        jobs.plan("out", 0, other + chunk(i))
        jobs.plan("out", 0, half + chunk(i))
    for kk in range(NKK):
        jobs.plan("hidden", 2, kk)
    for i in range(NK):
        jobs.plan("out", 2, other + i)
        jobs.plan("out", 2, half + i)

    back = {}
    parts = {}

    def piece(r, q, rel):
        return total.at[r, q, rows144(at.pairs[rel]), :]

    def from_y(q):
        return tok.at[0, q, 0:PAIR, :]

    def from_c(q):
        return tok.at[1, q, 0:PAIR, :]

    def send_y(i):
        q = chunk(i)
        back["y", i] = cp.remote(piece(0, q, 2), from_y(q), at.y)

    def send_c(i):
        q = chunk(i)
        back["c", i] = cp.remote(piece(0, q, 1), from_c(q), at.c)

    def add_cores(r, i, q):
        number = r * NK + i
        if number >= 2:
            parts[number - 2].wait_send()
        out_stage[number % 2] = jobs.run().astype(BF)
        parts[number] = cp.remote(out_stage.at[number % 2], part.at[q], at.mate)
        v = jobs.run()
        parts[number].wait_recv()
        total[r, q] = (v + part[q].astype(F32)).astype(BF)

    def add_backward(i):
        q = chunk(i)
        add_cores(0, i, q)
        if i < 2:
            back["g", i] = cp.remote(piece(0, q, 3), from_g.at[i], at.g)
            send_y(i)
            send_c(i)
        else:
            back["g", i - 2].wait_recv()
            pass_y[i - 2] = (
                total[0, q, rows144(at.pairs[3]), :].astype(F32) + from_g[i - 2].astype(F32)
            ).astype(BF)
            back["yg", i] = cp.remote(pass_y.at[i - 2], from_yc.at[i - 2, 0], at.c)

    def relay_back(i):
        back["yg", i].wait_recv()
        back["ygy", i] = cp.remote(from_yc.at[i - 2, 0], from_yc.at[i - 2, 1], at.y)

    def mix(terms):
        v = jnp.zeros((256, terms[0][2].shape[-1]), F32)
        for fb, rel, rr in terms:
            v = v + dot(weights[fb, rel, 0], rr)
            v = v + dot(weights[fb, rel, 1], rr)
        return v

    def combine_backward(i):
        q = chunk(i)
        back["y", i].wait_recv()
        back["c", i].wait_recv()
        terms = [
            (1, 0, total[0, q, rows144(at.pairs[0]), :]),
            (1, 1, from_c(q)[...]),
            (1, 2, from_y(q)[...]),
        ]
        if i >= 2:
            back["ygy", i].wait_recv()
            terms.append((1, 3, from_yc[i - 2, 1]))
        v = mix(terms)
        comb_own[q] = v[0:128]
        comb_out[q] = v[128:256].astype(BF)
        back["u", i] = cp.remote(comb_out.at[q], comb_in.at[q], at.g)

    def span(piece_):
        return slice(0, 512) if piece_ == 0 else slice(512, CH)

    def forward_c(i, side):
        return tok.at[2, i, 0:PAIR, :] if side == 0 else from_cf.at[i]

    def add_forward(i):
        add_cores(1, i, i)
        for p in range(2):
            for side in range(2):
                rows_ = rows144(at.pairs[1 + 2 * side])
                back["fc", i, p, side] = cp.remote(
                    total.at[1, i, rows_, span(p)], forward_c(i, side).at[:, span(p)], at.c)

    def combine_forward(i, p):
        for side in range(2):
            back["fc", i, p, side].wait_recv()
            v = mix([
                (0, 2 * side, total[1, i, rows144(at.pairs[2 * side]), span(p)]),
                (0, 2 * side + 1, forward_c(i, side)[:, span(p)]),
            ])
            both_own[i, side, :, span(p)] = v[0:128]
            m = 2 * i + side
            out = stage.at[m // 4, m % 4, 0:128, span(p)]
            out[...] = v[128:256].astype(BF)
            back["fu", i, p, side] = cp.remote(out, both_in.at[i, side, :, span(p)], at.g)

    def finish_forward(i, p):
        first = 0 if p == 0 else 512
        width = 512 if p == 0 else CH - 512
        for side in (1, 0):
            back["fu", i, p, side].wait_recv()
            v = both_own[i, side, :, span(p)] + both_in[i, side, :, span(p)].astype(F32)
            if side == 0:
                v = v + x_pair[:, i * CH + first:i * CH + first + width].astype(F32)
            v = v.astype(BF)
            target = yf_parts.at[
                2 * side, :, pl.ds(pl.multiple_of((half + i) * CH + first, 128), width)]
            to = (at.me, at.mate) if side == 0 else (at.y, at.ymate)
            section = up_s if side == 0 else beside_s
            for c in range(2):
                hbuf[side, 2 * i + c, :, span(p)] = v[c * 64:(c + 1) * 64]
            back["own", i, p, side] = cp.remote(
                hbuf.at[side, 2 * i + core, :, span(p)], target, to[0], section)
            back["mate", i, p, side] = cp.remote(
                hbuf.at[side, 2 * i + 1 - core, :, span(p)], target, to[1], section)

    def send_up(i, p):
        first = 0 if p == 0 else 512
        width = 512 if p == 0 else CH - 512
        ends = []
        for part_ in (half, other):
            cols = pl.ds(pl.multiple_of((part_ + i) * CH + first, 128), width)
            ends.append((cols, cp.sem(), cp.sem()))

        @pl.when(even)
        def _():
            for kind, (cols, send, recv) in zip(("own", "mate"), ends):
                back[kind, i, p, 1].wait_recv()
                pltpu.make_async_remote_copy(
                    src_ref=yf_parts.at[2, :, cols], dst_ref=yf_parts.at[1, :, cols],
                    send_sem=send, recv_sem=recv,
                    device_id=coordinates(at.me, up2_s), device_id_type=MESH,
                ).start()

        @pl.when(jnp.logical_not(even))
        def _():
            for kind in ("own", "mate"):
                back[kind, i, p, 1].wait_recv()

        return ends

    def wait_up(ends):
        @pl.when(even)
        def _():
            for cols, send, recv in ends:
                copy = pltpu.make_async_remote_copy(
                    src_ref=yf_parts.at[2, :, cols], dst_ref=yf_parts.at[1, :, cols],
                    send_sem=send, recv_sem=recv,
                    device_id=coordinates(at.me, up2_s), device_id_type=MESH,
                )
                copy.wait_send()
                copy.wait_recv()

    def finish_backward(i):
        q = chunk(i)
        back["u", (i + 2) % NK].wait_recv()
        v = comb_own[q] + comb_in[q].astype(F32)
        spread[q, 0] = v[0:64]
        spread[q, 1] = v[64:128]
        back["d", i] = cp.remote(spread.at[q, 1 - core], acc.at[half + q], at.mate)
        acc[half + q] = spread[q, core]

    def finalize_backward():
        for i in range(NK):
            back["d", i].wait_recv()
        along = jnp.zeros((TOK, 1), F32)
        for kk in range(NKK):
            cols = slice(kk * CH, (kk + 1) * CH)
            x = xin[0, :, cols].astype(F32)
            along = along + jnp.sum(x * (gain[:, cols] * acc[kk]), axis=-1, keepdims=True)
        inverse = scale[0]
        factor = inverse * inverse * inverse * (along / D)
        for kk in range(NKK):
            cols = slice(kk * CH, (kk + 1) * CH)
            x = xin[0, :, cols].astype(F32)
            v = xin[1, :, cols].astype(F32) + inverse * (gain[:, cols] * acc[kk]) - x * factor
            xin[2, :, cols] = v.astype(BF)
        back["s"] = cp.remote(xin.at[2], dx_out, at.me, down_s)

    def mixing_weights():
        meta_y.wait_recv()
        meta_t[...] = jnp.zeros_like(meta_t)
        for side in range(2):
            for w in range(2):
                hh = h if w == 0 else 1 - h
                meta_t[0:16, :] = metas[side, 2 * hh] + metas[side, 2 * hh + 1]
                m = jnp.transpose(meta_t[...])
                todo = [(0, 2 * side + rel, rel) for rel in range(2)]
                if side == 0:
                    todo = todo + [(1, rel, rel) for rel in range(4)]
                for fb, place, rel in todo:
                    first = at.pairs[rel] * PAIR
                    ids = (lax.broadcasted_iota(jnp.int32, (128, PAIR), 1) + first).astype(F32)
                    c = fb * 8
                    v = jnp.where(ids == m[:, c:c + 1], m[:, c + 2:c + 3], 0.0)
                    v = v + jnp.where(ids == m[:, c + 1:c + 2], m[:, c + 3:c + 4], 0.0)
                    high = v.astype(BF)
                    weights[fb, place, 0, w * 128:(w + 1) * 128, :] = high
                    weights[fb, place, 1, w * 128:(w + 1) * 128, :] = (
                        v - high.astype(F32)).astype(BF)

    def run(count):
        for _ in range(count):
            jobs.run()

    for s in range(n + 3):
        if s > 0:
            send_tokens(s + 2)
        if s >= 3:
            for m in tok_g[s - 3]:
                m.wait_send()
        if s < n:
            gather(s)
        relay_first(s - 1)
        if s == n - 1:
            add_backward(0)
        relay_second(s - 2)
        pass_on(s - 2)
        if s >= n:
            add_backward(s - 11)
        relay_last(s - 3)
        pass_extra(s - 4)
        if s == 4:
            placing(0)
            mixing_weights()
        if s == 6:
            complete(0)
        if s in (6, 7):
            run(3)
        if s == 8:
            run(2)
        if s == 9:
            complete(1)
        if s in (9, 10):
            run(4)
    complete(2)
    send_c(2)
    send_y(2)
    send_c(3)
    send_y(3)
    run(3)
    relay_back(2)
    combine_backward(0)
    run(3)
    relay_back(3)
    combine_backward(1)
    run(2)
    for (s, rel), m in sent.items():
        if s >= n - 3:
            m.wait_send()
    for m in tok_in + [x_in]:
        m.wait_send()
    x_in.wait_recv()
    x_own.wait()
    add_forward(0)
    combine_backward(2)
    add_forward(1)
    combine_backward(3)
    finish_backward(2)
    finish_backward(3)
    combine_forward(0, 0)
    add_forward(2)
    finish_backward(0)
    finish_backward(1)
    combine_forward(0, 1)
    finalize_backward()
    add_forward(3)
    gone = []
    combine_forward(1, 0)
    finish_forward(0, 0)
    combine_forward(1, 1)
    finish_forward(0, 1)
    gone.append(send_up(0, 0))
    combine_forward(2, 0)
    finish_forward(1, 0)
    gone.append(send_up(0, 1))
    combine_forward(2, 1)
    finish_forward(1, 1)
    gone.append(send_up(1, 0))
    combine_forward(3, 0)
    finish_forward(2, 0)
    gone.append(send_up(1, 1))
    combine_forward(3, 1)
    finish_forward(2, 1)
    gone.append(send_up(2, 0))
    finish_forward(3, 0)
    gone.append(send_up(2, 1))
    finish_forward(3, 1)
    gone.append(send_up(3, 0))
    gone.append(send_up(3, 1))

    assert cp.used <= ENDS, cp.used
    for m in meta_sends + [meta_y] + list(passed.values()):
        m.wait_send()
    for number in (2 * NK - 2, 2 * NK - 1):
        parts[number].wait_send()
    for m in back.values():
        m.wait_send()
    back["s"].wait_recv()
    for key, m in back.items():
        if key[0] in ("own", "mate") and key[3] == 0:
            m.wait_recv()
    for ends in gone:
        wait_up(ends)


def relay(x_fwd, x_bwd, cot, gain, tables, wg, wu, wd):
    vmem = pl.BlockSpec(memory_space=pltpu.VMEM)
    hbm = pl.BlockSpec(memory_space=pl.ANY)
    arrived_parts, returned, _ = pl.pallas_call(
        relay_kernel,
        out_shape=(
            jax.ShapeDtypeStruct((3, TOK, D), BF),
            jax.ShapeDtypeStruct((TOK, D), BF),
            jax.ShapeDtypeStruct((3, NKK, SLOTS, CH), BF),
        ),
        in_specs=[hbm] * 3 + [vmem] * 7 + [hbm] * 3,
        out_specs=(hbm, hbm, hbm),
        scratch_shapes=[
            pltpu.VMEM((3, TOK, D), BF),
            pltpu.VMEM((3, NKK, TOK, CH), BF),
            pltpu.VMEM((128, NK * CH), BF),
            pltpu.VMEM((3, NK, 256, CH), BF),
            pltpu.VMEM((3, 4, PAIR, CH), BF),
            pltpu.VMEM((3, 2, PAIR, CH), BF),
            pltpu.VMEM((2, 4, 16, 128), F32),
            pltpu.VMEM((2, 4, PAIR, 256), BF),
            pltpu.VMEM((128, 128), F32),
            pltpu.VMEM((2, 4, 2, 256, PAIR), BF),
            pltpu.VMEM((NK, SLOTS, CH), BF),
            pltpu.VMEM((2, NK, SLOTS, CH), BF),
            pltpu.VMEM((NK, PAIR, CH), BF),
            pltpu.VMEM((2, PAIR, CH), BF),
            pltpu.VMEM((2, PAIR, CH), BF),
            pltpu.VMEM((2, 2, PAIR, CH), BF),
            pltpu.VMEM((NK, 128, CH), F32),
            pltpu.VMEM((NK, 128, CH), BF),
            pltpu.VMEM((NK, 128, CH), BF),
            pltpu.VMEM((NK, 2, TOK, CH), F32),
            pltpu.VMEM((NKK, TOK, CH), F32),
            pltpu.VMEM((NK, 2, 128, CH), F32),
            pltpu.VMEM((NK, 2, 128, CH), BF),
            pltpu.VMEM((2, SLOTS, CH), BF),
            pltpu.VMEM((2, SLOTS, CH), BF),
            pltpu.VMEM((2, CH, HID), BF),
            pltpu.VMEM((2, CH, HID), BF),
            pltpu.VMEM((2, HID, CH), BF),
            pltpu.VMEM((SLOTS, HID), F32),
            pltpu.VMEM((SLOTS, HID), F32),
            pltpu.VMEM((SLOTS, HID), F32),
            pltpu.VMEM((SLOTS, HID), BF),
            pltpu.VMEM((SLOTS, HID), BF),
            pltpu.VMEM((SLOTS, HID), BF),
            pltpu.SemaphoreType.DMA((ENDS,)),
        ],
        compiler_params=pltpu.CompilerParams(
            collective_id=1, has_side_effects=True, vmem_limit_bytes=64 * 2 ** 20),
        name="relay",
    )(x_fwd, x_bwd, cot, gain, *tables, wg, wu, wd)
    odd = lax.rem(lax.axis_index("section"), 2) == 1
    across = jnp.where(odd, arrived_parts[2], arrived_parts[1])
    arrived = arrived_parts[0].astype(F32) + across.astype(F32)
    return arrived.astype(BF), returned


def on_device(
    x_fwd, routes_fwd, slots_fwd, logits_fwd,
    x_bwd, cot_bwd, routes_bwd, slots_bwd, logits_bwd,
    gain, w_gate, w_up, w_down,
):
    tables = [
        v[0].T for v in (
            routes_fwd, slots_fwd, logits_fwd, routes_bwd, slots_bwd, logits_bwd)
    ]
    arrived, returned = relay(
        x_fwd[0], x_bwd[0], cot_bwd[0], gain, tables, w_gate[0], w_up[0], w_down[0])
    return (arrived[None], returned[None])


def solution(mesh):
    return jax.shard_map(
        on_device,
        mesh=mesh,
        in_specs=(
            P("section", "expert", None),
            P("section", "expert", None),
            P("section", "expert", None),
            P("section", "expert", None),
            P("section", "expert", None),
            P("section", "expert", None),
            P("section", "expert", None),
            P("section", "expert", None),
            P("section", "expert", None),
            P("section", None),
            P("section", None, "expert"),
            P("section", None, "expert"),
            P("section", "expert", None),
        ),
        out_specs=(P("section", "expert", None), P("section", "expert", None)),
        check_vma=False,
    )
```
